128 devices in a mesh: star: 8 (over y, core), tm: 16 (over x, z).
Axes of the slice: x: 4, y: 4, z: 4, core: 2. Of those that a mesh axis runs over, the one named last changes fastest.
Arguments:
- flux: float32 [16384, 8192], P('star', 'tm'), may hold values from -6 to 6
- valid: int32 [16384, 8192], P('star', 'tm'), may hold values 0 or 1
- quality: int32 [16384, 8192], P('star', 'tm'), may hold values from 0 to 3
- basis: float32 [16, 8192], P(None, 'tm'), may hold values from -0.0625 to 0.0625
- neighbours: int32 [16384, 64], P('star'), may hold values from 0 to 16383
- prior_prec: float32 [16], replicated, may hold values from 0.3 to 3
- decay: float32 [16, 8192], P(None, 'tm'), may hold values from 0.3 to 1, as said below
- load_u: float32 [16, 8192], P(None, 'tm'), may hold values from -1.5 to 1.5
- feed_w: float32 [16, 8192], P(None, 'tm'), may hold values from -0.0625 to 0.0625
- inv_diag: float32 [8192], P('tm'), may hold values from 0.25 to 1.75
Outputs:
- map_coeffs: float32 [16384, 16], P('star')
- whitened: float32 [16384, 8192], P('star', 'tm')
The draws below stay inside these ranges and needn't reach their ends.
Inputs may be any that keep to these rules, and one draw needn't show every extreme that they name: `decay`: each factor is positive and at most 1.
All inputs are finite; a program needn't handle non-finite values. No bound on the sum of `valid` on one device may be relied on, other than what follows from the above.
Results may differ from the reference program's by a relative error of at most 0.00011.
Values sent between devices are 32-bit elements; how exact they have to be, the bound alone decides.
No kernel may reach another device: no remote copies, remote signals or barrier semaphores. Data moves between devices by JAX's collectives and lax.ppermute only.
A program may use at most 256 MiB of HBM per device.

```python
import math
import jax
import jax.numpy as jnp
from jax import lax

BASIS_VECTORS = 16
NOISE_TERMS = 16
NEIGH = 64
STARS = 16384
CADENCE_COUNT = 8192


def draw_decay(key, part):
    random_keys = jax.random.split(key, 7)
    fast_share = 0.5
    fast_pick = jax.random.uniform(random_keys[0], (NOISE_TERMS,)) < fast_share
    fast_rate = jax.random.uniform(random_keys[1], (NOISE_TERMS,), minval=1.0 / 50.0, maxval=1.0 / 30.0)
    slow_rate = jax.random.uniform(random_keys[2], (NOISE_TERMS,), minval=0.1, maxval=0.9) / CADENCE_COUNT
    base_rate = jnp.where(fast_pick, fast_rate, slow_rate)
    phase_shift = jax.random.uniform(random_keys[3], (NOISE_TERMS,), minval=0.0, maxval=6.2831853)
    cadence_position = jnp.arange(CADENCE_COUNT).astype(jnp.float32)
    rate_swing = jnp.exp(0.7 * jnp.sin(6.2831853 * 3.0 * cadence_position[None, :] / CADENCE_COUNT + phase_shift[:, None]))
    jitter = jax.random.uniform(random_keys[4], (NOISE_TERMS, CADENCE_COUNT), minval=0.7, maxval=1.3)
    smooth_component = jnp.exp(-base_rate[:, None] * rate_swing * jitter)
    outlier_locations = jax.random.randint(random_keys[5], (2,), 0, CADENCE_COUNT)
    outlier_mask = jnp.any(jnp.arange(CADENCE_COUNT)[None, :] == outlier_locations[:, None], axis=0)
    outlier_keep = jax.random.uniform(random_keys[6], (NOISE_TERMS, CADENCE_COUNT), minval=0.6, maxval=0.8)
    return (smooth_component * jnp.where(outlier_mask[None, :], outlier_keep, 1.0)).astype(jnp.float32)


def with_ends(array, key, smallest, top_value):
    place = [jax.random.randint(jax.random.fold_in(key, axis), (), 0, length) for axis, length in enumerate(array.shape)]
    widest = array.shape.index(max(array.shape))
    next_to = place[:widest] + [(place[widest] + 1) % array.shape[widest]] + place[widest + 1:]
    return array.at[tuple(place)].set(smallest).at[tuple(next_to)].set(top_value)


def block_scale(own_key, dims, cuts, smallest, high):
    def one(position, shards_of):
        draws = jax.random.uniform(jax.random.fold_in(jax.random.fold_in(own_key, 6), position), (shards_of,), jnp.float32, smallest / len(cuts), high / len(cuts))
        return jnp.repeat(jnp.exp(draws), dims[position] // shards_of).reshape((-1,) + (1,) * (len(dims) - position - 1))

    loudness = one(*cuts[0])
    for cut in cuts[1:]:
        loudness = loudness * one(*cut)
    return loudness


def bell_draw(key, extent, scale, bound, pieces=(), held_as=jnp.bfloat16):
    values = scale * jax.random.normal(key, extent, jnp.float32)
    if pieces:
        values = values * block_scale(key, extent, pieces, -0.22, 0.18)
    return jnp.clip(values, -bound, bound).astype(held_as)


def setup_inputs(seed: int = 0) -> dict:
    key_of = jax.random.split(jax.random.key(seed), 11)
    flux = bell_draw(key_of[0], (STARS, CADENCE_COUNT), 1.0, 6.0, ((0, 8), (1, 16)), jnp.float32)
    valid = with_ends((jax.random.randint(key_of[1], (STARS, CADENCE_COUNT), 0, 10) < 9).astype(jnp.int32), jax.random.fold_in(key_of[1], 1), 0, 1)
    quality = with_ends(jax.random.randint(key_of[2], (STARS, CADENCE_COUNT), 0, 4), jax.random.fold_in(key_of[2], 1), 0, 3).astype(jnp.int32)
    basis = bell_draw(key_of[3], (BASIS_VECTORS, CADENCE_COUNT), CADENCE_COUNT ** -0.5, 0.0625, ((1, 16),), jnp.float32)
    neighbours = with_ends(jax.random.randint(key_of[4], (STARS, NEIGH), 0, STARS), jax.random.fold_in(key_of[4], 1), 0, STARS - 1).astype(jnp.int32)
    prior_prec = jnp.clip(jnp.exp(jax.random.uniform(key_of[5], (BASIS_VECTORS,), jnp.float32, math.log(0.3), math.log(3.0))), 0.3, 3.0)
    decay = draw_decay(jax.random.fold_in(key_of[10], 71), 0)
    load_u = bell_draw(key_of[7], (NOISE_TERMS, CADENCE_COUNT), NOISE_TERMS ** -0.5, 1.5, ((1, 16),), jnp.float32)
    feed_w = bell_draw(key_of[8], (NOISE_TERMS, CADENCE_COUNT), CADENCE_COUNT ** -0.5, 0.0625, ((1, 16),), jnp.float32)
    inv_diag = jnp.clip(1.0 + 0.15 * jax.random.normal(key_of[9], (CADENCE_COUNT,), jnp.float32), 0.25, 1.75)
    return dict(flux=flux, valid=valid, quality=quality, basis=basis, neighbours=neighbours, prior_prec=prior_prec, decay=decay, load_u=load_u, feed_w=feed_w, inv_diag=inv_diag)


HIGHEST = lax.Precision.HIGHEST

def spd_solve(matrix, vector):
    order = matrix.shape[-1]
    factor = [[None] * order for index in range(order)]
    for column in range(order):
        pivot = matrix[:, column, column]
        for inner in range(column):
            pivot = pivot - factor[column][inner] * factor[column][inner]
        root_value = jnp.sqrt(pivot)
        factor[column][column] = root_value
        for row_index in range(column + 1, order):
            entry = matrix[:, row_index, column]
            for inner in range(column):
                entry = entry - factor[row_index][inner] * factor[column][inner]
            factor[row_index][column] = entry / root_value
    forward = []
    for row_index in range(order):
        entry = vector[:, row_index]
        for inner in range(row_index):
            entry = entry - factor[row_index][inner] * forward[inner]
        forward.append(entry / factor[row_index][row_index])
    backward = [None] * order
    for row_index in range(order - 1, -1, -1):
        entry = forward[row_index]
        for inner in range(row_index + 1, order):
            entry = entry - factor[inner][row_index] * backward[inner]
        backward[row_index] = entry / factor[row_index][row_index]
    return jnp.stack(backward, axis=1)

def reference(flux, valid, quality, basis, neighbours, prior_prec, decay, load_u, feed_w, inv_diag):
    valid_f = valid.astype(jnp.float32)
    weight = valid_f / (1.0 + quality.astype(jnp.float32))
    paired_rows = (basis[:, None, :] * basis[None, :, :]).reshape(BASIS_VECTORS * BASIS_VECTORS, CADENCE_COUNT)
    gram_sums = lax.dot_general(weight, paired_rows, (((1,), (1,)), ((), ())), precision=HIGHEST)
    right_sums = lax.dot_general(weight * flux, basis, (((1,), (1,)), ((), ())), precision=HIGHEST)
    matrices = gram_sums.reshape(STARS, BASIS_VECTORS, BASIS_VECTORS)
    fitted = spd_solve(matrices + 0.1 * jnp.eye(BASIS_VECTORS, dtype=jnp.float32), right_sums)
    prior_mean = lax.optimization_barrier(jnp.mean(jnp.take(fitted, neighbours, axis=0), axis=1))
    map_coeffs = spd_solve(matrices + jnp.diag(prior_prec), right_sums + prior_prec[None, :] * prior_mean)
    residual = valid_f * (flux - jnp.dot(map_coeffs, basis, precision=HIGHEST))

    def advance(carry_state, inputs):
        flux_now, decay_now, load_now, feed_now, scale_now = inputs
        output_now = (flux_now - lax.optimization_barrier(jnp.sum(carry_state * load_now[None, :], axis=1))) * scale_now
        carry_state = carry_state * decay_now[None, :] + flux_now[:, None] * feed_now[None, :]
        return (carry_state, output_now)
    start_state = jnp.zeros((STARS, NOISE_TERMS), jnp.float32)
    final_state, outputs = lax.scan(advance, start_state, (residual.T, decay.T, load_u.T, feed_w.T, inv_diag))
    return (map_coeffs, outputs.T)
```

```python
import jax
import jax.numpy as jnp
import numpy as np
from jax import lax
from jax.experimental import pallas as pl
from jax.experimental.pallas import tpu as pltpu
from jax.sharding import Mesh, PartitionSpec as P

BASIS_VECTORS = 16
NOISE_TERMS = 16
NEIGH = 64
DIAGONALS = 9
PAIRS = 136
OWN = 128
CUT = 128
STEP = 256
CHUNKS = STEP // OWN
GRAM_ROWS = PAIRS + 16
CROSS_ROWS = 16 + BASIS_VECTORS * NOISE_TERMS
WHITEN_STEP = 512
WHITEN_CHUNKS = WHITEN_STEP // OWN

F32 = jnp.float32
BF16 = jnp.bfloat16
MIB = 1 << 20


def split3(x):
    high = x.astype(BF16)
    rest = x - high.astype(F32)
    mid = rest.astype(BF16)
    low = (rest - mid.astype(F32)).astype(BF16)
    return high, mid, low


def left_stack(x):
    high, mid, low = split3(x)
    return jnp.concatenate([high, high, mid, high, mid, low], axis=0)


def right_stack(x):
    high, mid, low = split3(x)
    return jnp.concatenate([high, mid, high, low, mid, high], axis=0)


def dot_nt(a, b):
    return lax.dot_general(a, b, (((1,), (1,)), ((), ())), preferred_element_type=F32)


def dot_tn(a, b):
    return lax.dot_general(a, b, (((0,), (0,)), ((), ())), preferred_element_type=F32)


def dot_nn(a, b):
    return lax.dot_general(a, b, (((1,), (0,)), ((), ())), preferred_element_type=F32)


def masked_sums(x, mask):
    rows = x.shape[0]
    stacked = jnp.concatenate(split3(x), axis=0)
    sums = dot_nn(stacked, mask.astype(F32).astype(BF16))
    return sums[0:rows] + (sums[rows : 2 * rows] + sums[2 * rows : 3 * rows])


def narrow_dots(table_ref, start, x, pieces):
    parts = split3(x)[:pieces]
    sums = [
        dot_nt(table_ref[start : start + 16 * (3 - place), :], part)
        for place, part in enumerate(parts)
    ]
    total = sums[0][32:48]
    for place in range(1, pieces):
        total = total + sums[place][16 * (2 - place) : 16 * (3 - place)]
    mid = sums[0][16:32] + sums[1][0:16]
    return sums[0][0:16] + (mid + total)


def gram_kernel(flux_ref, valid_ref, quality_ref, basis_ref, out_ref, marked_ref, table_ref):
    wide = DIAGONALS * BASIS_VECTORS
    rights = 3 * wide

    @pl.when(pl.program_id(0) == 0)
    def _():
        basis = basis_ref[...]
        scaled = basis * (1.0 / 12.0)
        products = []
        for diagonal in range(DIAGONALS):
            turned = basis
            if diagonal:
                turned = jnp.concatenate([basis[diagonal:], basis[:diagonal]], axis=0)
            products.append(scaled * turned)
        for place, piece in enumerate(split3(jnp.concatenate(products, axis=0))):
            table_ref[place * wide : (place + 1) * wide, :] = piece
        for place, piece in enumerate(split3(scaled)):
            table_ref[rights + place * 16 : rights + place * 16 + 16, :] = piece

    flux = flux_ref[...]
    quality = quality_ref[...]
    usable = valid_ref[...] != 0
    marked_ref[...] = jnp.where(usable, flux, jnp.nan)
    twelfths = jnp.where(
        quality == 0, 12.0, jnp.where(quality == 1, 6.0, jnp.where(quality == 2, 4.0, 3.0))
    )
    weight = jnp.where(usable, twelfths, 0.0)
    grams = dot_nt(table_ref[0:rights, :], weight.astype(BF16))
    gram = grams[0:PAIRS] + (grams[wide : wide + PAIRS] + grams[2 * wide : 2 * wide + PAIRS])
    right = narrow_dots(table_ref, rights, weight * flux, 3)
    for chunk in range(CHUNKS):
        lanes = slice(chunk * OWN, (chunk + 1) * OWN)
        out_ref[chunk, 0:PAIRS, :] = gram[:, lanes]
        out_ref[chunk, PAIRS:GRAM_ROWS, :] = right[:, lanes]


def cross_kernel(marked_ref, basis_ref, decay_ref, feed_ref, out_ref, decayed_ref, table_ref):
    cross = BASIS_VECTORS * NOISE_TERMS
    feeds = 2 * cross

    @pl.when(pl.program_id(0) == 0)
    def _():
        log_decay = jnp.log(decay_ref[...])
        count = log_decay.shape[1]
        rows = lax.broadcasted_iota(jnp.int32, (count, count), 0)
        columns = lax.broadcasted_iota(jnp.int32, (count, count), 1)
        suffix = masked_sums(log_decay, rows > columns)
        feed = jnp.exp(suffix) * feed_ref[...]
        whole = jnp.exp(suffix[:, 0:1] + log_decay[:, 0:1])
        decayed_ref[...] = jnp.broadcast_to(whole, (NOISE_TERMS, OWN))
        for k in range(BASIS_VECTORS):
            product = basis_ref[k : k + 1, :] * feed
            for place, piece in enumerate(split3(product)[:2]):
                first = place * cross + k * 16
                table_ref[first : first + 16, :] = piece
        for place, piece in enumerate(split3(feed)):
            table_ref[feeds + place * 16 : feeds + place * 16 + 16, :] = piece

    marked = marked_ref[...]
    usable = marked == marked
    sums = dot_nt(table_ref[0:feeds, :], jnp.where(usable, 1.0, 0.0).astype(BF16))
    crossed = sums[0:cross] + sums[cross : 2 * cross]
    plain = narrow_dots(table_ref, feeds, jnp.where(usable, marked, 0.0), 2)
    for chunk in range(CHUNKS):
        lanes = slice(chunk * OWN, (chunk + 1) * OWN)
        out_ref[chunk, 0:16, :] = plain[:, lanes]
        out_ref[chunk, 16:CROSS_ROWS, :] = crossed[:, lanes]


def count_kernel(code_ref, low_ref, out_ref):
    entries = 8 * NEIGH
    row_code = lax.broadcasted_iota(jnp.int32, (128 * 8, entries), 0)
    low_code = lax.broadcasted_iota(jnp.int32, (128, entries), 0)

    def one_half(group):
        code = code_ref[pl.ds(group, 1), :]
        low = low_ref[pl.ds(group, 1), :]
        highs = jnp.where(row_code == code, 1.0, 0.0).astype(BF16)
        lows = jnp.where(low_code == low, 1.0, 0.0).astype(BF16)
        return dot_nt(highs, lows).reshape(128, 8, 128)

    def one(step, ignored):
        both = jnp.concatenate([one_half(2 * step), one_half(2 * step + 1)], axis=1)
        out_ref[:, pl.ds(pl.multiple_of(step * 16, 16), 16), :] = both.astype(BF16)
        return ignored

    lax.fori_loop(0, OWN // 16, one, 0)


def noise_kernel(
    decay_ref, load_ref, feed_ref, basis_ref, high_ref, low_ref, entry_ref, stack_ref
):
    log_decay = jnp.log(decay_ref[...])
    load = load_ref[...]
    feed = feed_ref[...]
    count = log_decay.shape[1]
    rows = lax.broadcasted_iota(jnp.int32, (count, count), 0)
    columns = lax.broadcasted_iota(jnp.int32, (count, count), 1)
    together = (rows // CUT) == (columns // CUT)
    before = masked_sums(log_decay, together & (rows < columns))
    tail = masked_sums(log_decay, together & (rows > columns))
    through = before + log_decay
    cuts = count // CUT
    totals = [through[:, (cut + 1) * CUT - 1 : (cut + 1) * CUT] for cut in range(cuts)]
    lower = lax.broadcasted_iota(jnp.int32, (CUT, CUT), 0) < lax.broadcasted_iota(
        jnp.int32, (CUT, CUT), 1
    )
    high_ref[...] = jnp.zeros_like(high_ref)
    low_ref[...] = jnp.zeros_like(low_ref)

    def keep(u, t, block):
        high = block.astype(BF16)
        span = (slice(u * CUT, (u + 1) * CUT), slice(t * CUT, (t + 1) * CUT))
        high_ref[span] = high
        low_ref[span] = (block - high.astype(F32)).astype(BF16)

    passed = jnp.zeros((NOISE_TERMS, 1), F32)
    entries = []
    for t in range(cuts):
        lanes = slice(t * CUT, (t + 1) * CUT)
        middle = through[:, t * CUT + CUT // 2 - 1 : t * CUT + CUT // 2]
        near_left = feed[:, lanes] * jnp.exp(middle - through[:, lanes])
        near_right = load[:, lanes] * jnp.exp(before[:, lanes] - middle)
        near = dot_tn(left_stack(near_left), right_stack(near_right))
        keep(t, t, jnp.where(lower, near, 0.0))
        far_right = right_stack(load[:, lanes] * jnp.exp(before[:, lanes]))
        between = jnp.zeros((NOISE_TERMS, 1), F32)
        for u in range(t - 1, -1, -1):
            span = slice(u * CUT, (u + 1) * CUT)
            far_left = left_stack(feed[:, span] * jnp.exp(tail[:, span] + between))
            keep(u, t, dot_tn(far_left, far_right))
            between = between + totals[u]
        entries.append(load[:, lanes] * jnp.exp(before[:, lanes] + passed))
        passed = passed + totals[t]
    entry_ref[...] = right_stack(jnp.concatenate(entries, axis=1))
    stack_ref[...] = right_stack(basis_ref[...])


def row_of_pair(i, j):
    apart = (j - i) % BASIS_VECTORS
    if apart < 8 or (apart == 8 and i < 8):
        return apart * BASIS_VECTORS + i
    return ((i - j) % BASIS_VECTORS) * BASIS_VECTORS + j


def eliminate(columns, vector):
    order = BASIS_VECTORS
    columns = list(columns)
    rows = lax.broadcasted_iota(jnp.int32, columns[0].shape, 0)
    scaled, pivots = [], []
    for k in range(order):
        inverse = 1.0 / columns[k][k : k + 1, :]
        factor = jnp.where(rows > k, columns[k] * inverse, 0.0)
        for j in range(k + 1, order):
            columns[j] = columns[j] - factor * columns[j][k : k + 1, :]
        scaled.append(factor)
        pivots.append(inverse)
        if vector is not None:
            vector = vector - factor * vector[k : k + 1, :]
    return scaled, pivots, vector, columns


def back_substitute(vector, uppers, pivots):
    rows = lax.broadcasted_iota(jnp.int32, vector.shape, 0)
    solved = jnp.zeros_like(vector)
    for k in range(BASIS_VECTORS - 1, -1, -1):
        value = vector[k : k + 1, :] * pivots[k]
        vector = vector - uppers[k] * value
        solved = jnp.where(rows == k, value, solved)
    return solved


def solve_kernel(parts_ref, prec_ref, fitted_ref, factor_ref, upper_ref, pivot_ref, right_ref, sums_ref, matrix_ref):
    total = parts_ref[0]
    for part in range(1, parts_ref.shape[0]):
        total = total + parts_ref[part]
    sums_ref[...] = total
    right = total[PAIRS : PAIRS + 16]
    right_ref[...] = right
    order = BASIS_VECTORS
    for j in range(order):
        for i in range(order):
            row = row_of_pair(i, j)
            matrix_ref[j * order + i : j * order + i + 1, :] = sums_ref[row : row + 1, :]
    rows = lax.broadcasted_iota(jnp.int32, right.shape, 0)
    plain = [matrix_ref[j * order : (j + 1) * order, :] for j in range(order)]
    prec = prec_ref[...]
    ridged = [jnp.where(rows == j, plain[j] + 0.1, plain[j]) for j in range(order)]
    ignored, pivots, reduced, uppers = eliminate(ridged, right)
    fitted = back_substitute(reduced, uppers, pivots)
    for peer in range(fitted_ref.shape[0]):
        fitted_ref[peer] = fitted
    weighted = [jnp.where(rows == j, plain[j] + prec, plain[j]) for j in range(order)]
    factors, pivots, ignored, uppers = eliminate(weighted, None)
    for k in range(order):
        factor_ref[k] = factors[k]
        upper_ref[k] = uppers[k]
        pivot_ref[k : k + 1, :] = pivots[k]


def map_kernel(
    fitted_ref, counts_ref, prec_ref, factor_ref, upper_ref, pivot_ref, right_ref, out_ref
):
    prior = jnp.zeros((48, OWN), F32)
    for place in range(0, fitted_ref.shape[0], 2):
        wide = jnp.concatenate([fitted_ref[place], fitted_ref[place + 1]], axis=1)
        listed = jnp.concatenate([counts_ref[place], counts_ref[place + 1]], axis=1)
        prior = prior + dot_nt(jnp.concatenate(split3(wide), axis=0), listed)
    prior_mean = (prior[0:16] + (prior[16:32] + prior[32:48])) * (1.0 / NEIGH)
    vector = right_ref[...] + prec_ref[...] * prior_mean
    for k in range(BASIS_VECTORS):
        vector = vector - factor_ref[k] * vector[k : k + 1, :]
    uppers = [upper_ref[k] for k in range(BASIS_VECTORS)]
    pivots = [pivot_ref[k : k + 1, :] for k in range(BASIS_VECTORS)]
    coeffs = back_substitute(vector, uppers, pivots)
    for peer in range(out_ref.shape[0]):
        out_ref[peer] = coeffs


def carry_kernel(rows_ref, crossed_ref, decayed_ref, out_ref):
    for owner in range(rows_ref.shape[0]):
        coeffs = rows_ref[owner]
        carry = crossed_ref[owner, 0:16, :]
        for k in range(BASIS_VECTORS):
            first = 16 + 16 * k
            carry = carry - coeffs[k : k + 1, :] * crossed_ref[owner, first : first + 16, :]
        out_ref[owner, 0:16, :] = carry
        out_ref[owner, 16:32, :] = decayed_ref[...]


def state_kernel(carry_ref, out_ref):
    state = jnp.zeros((NOISE_TERMS, OWN), F32)
    for block in range(carry_ref.shape[0]):
        out_ref[block] = state
        state = state * carry_ref[block, 16:32, :] + carry_ref[block, 0:16, :]


def local_kernel(marked_ref, rows_ref, stack_ref, high_ref, low_ref, coeffs_ref, out_ref):
    coeffs = jnp.concatenate([rows_ref[chunk] for chunk in range(WHITEN_CHUNKS)], axis=1)
    coeffs_ref[...] = coeffs
    trend = dot_tn(left_stack(coeffs), stack_ref[...])
    marked = marked_ref[...]
    residual = jnp.where(marked == marked, marked - trend, 0.0)
    high = residual.astype(BF16)
    low = (residual - high.astype(F32)).astype(BF16)
    count = residual.shape[1]
    for first in range(0, count, 256):
        lanes = slice(first, first + 256)
        upto = slice(0, first + 256)
        local = dot_nn(low[:, upto], high_ref[upto, lanes]) + dot_nn(high[:, upto], low_ref[upto, lanes])
        local = local + dot_nn(high[:, upto], high_ref[upto, lanes])
        out_ref[:, lanes] = residual[:, lanes] - local


def finish_kernel(local_ref, states_ref, entry_ref, scale_ref, out_ref):
    states = jnp.concatenate([states_ref[chunk] for chunk in range(WHITEN_CHUNKS)], axis=1)
    incoming = dot_tn(left_stack(states), entry_ref[...])
    out_ref[...] = (local_ref[...] - incoming) * scale_ref[...]


def vmem():
    return pl.BlockSpec(memory_space=pltpu.VMEM)


def params(mib):
    return pltpu.CompilerParams(vmem_limit_bytes=mib * MIB)


def cost(flops, bytes_accessed):
    return pl.CostEstimate(flops=flops, bytes_accessed=bytes_accessed, transcendentals=0)


def per_device(
    flux, valid, quality, basis, neighbours, prior_prec, decay, load_u, feed_w, inv_diag
):
    stars, cadences = flux.shape
    blocks = stars // OWN
    steps = stars // STEP
    place = lax.axis_index("tm")
    prec = jnp.broadcast_to(prior_prec[:, None], (BASIS_VECTORS, OWN))

    listed = lax.dynamic_slice_in_dim(neighbours, place * OWN, OWN, 0).reshape(blocks, -1)
    code = (listed >> 7) * 8 + lax.broadcasted_iota(jnp.int32, listed.shape, 1) // NEIGH

    wide_spec = pl.BlockSpec((STEP, cadences), lambda i: (i, 0))
    table_spec = pl.BlockSpec((16, cadences), lambda i: (0, 0))
    parts, marked = pl.pallas_call(
        gram_kernel,
        grid=(steps,),
        in_specs=[wide_spec, wide_spec, wide_spec, table_spec],
        out_specs=[pl.BlockSpec((CHUNKS, GRAM_ROWS, OWN), lambda i: (i, 0, 0)), wide_spec],
        out_shape=[
            jax.ShapeDtypeStruct((blocks, GRAM_ROWS, OWN), F32),
            jax.ShapeDtypeStruct((stars, cadences), F32),
        ],
        scratch_shapes=[pltpu.VMEM((480, cadences), BF16)],
        compiler_params=params(56),
        cost_estimate=cost(2 * stars * cadences * 600, 18 * MIB),
        name="gram",
    )(flux, valid, quality, basis)

    crossed, decayed = pl.pallas_call(
        cross_kernel,
        grid=(steps,),
        in_specs=[wide_spec, table_spec, table_spec, table_spec],
        out_specs=[
            pl.BlockSpec((CHUNKS, CROSS_ROWS, OWN), lambda i: (i, 0, 0)),
            pl.BlockSpec((NOISE_TERMS, OWN), lambda i: (0, 0)),
        ],
        out_shape=[
            jax.ShapeDtypeStruct((blocks, CROSS_ROWS, OWN), F32),
            jax.ShapeDtypeStruct((NOISE_TERMS, OWN), F32),
        ],
        scratch_shapes=[pltpu.VMEM((560, cadences), BF16)],
        compiler_params=params(56),
        cost_estimate=cost(2 * stars * cadences * 800, 8 * MIB),
        name="cross",
    )(marked, basis, decay, feed_w)
    parts = lax.all_to_all(parts, "tm", 0, 0, tiled=True)
    parts, crossed, decayed = lax.optimization_barrier((parts, crossed, decayed))

    square = jax.ShapeDtypeStruct((16, 16, OWN), F32)
    flat = jax.ShapeDtypeStruct((16, OWN), F32)
    everyone = ("y", "c", "tm")
    copies = jax.ShapeDtypeStruct((lax.axis_size(everyone), 16, OWN), F32)
    fitted, factor, upper, pivot, right = pl.pallas_call(
        solve_kernel,
        in_specs=[vmem()] * 2,
        out_specs=[vmem()] * 5,
        out_shape=[copies, square, square, flat, flat],
        scratch_shapes=[pltpu.VMEM((GRAM_ROWS, OWN), F32), pltpu.VMEM((256, OWN), F32)],
        compiler_params=params(16),
        cost_estimate=cost(1 << 20, 2 * MIB),
        name="solve",
    )(parts, prec)

    fitted, later_code, later_low, later_decay, later_basis = lax.optimization_barrier(
        (fitted, code, listed & 127, decay, basis)
    )
    fitted = lax.all_to_all(fitted, everyone, 0, 0, tiled=True)
    counts = pl.pallas_call(
        count_kernel,
        in_specs=[vmem(), vmem()],
        out_specs=vmem(),
        out_shape=jax.ShapeDtypeStruct((128, OWN, 128), BF16),
        compiler_params=params(16),
        cost_estimate=cost(4 << 30, 4 * MIB),
        name="count",
    )(later_code, later_low)
    high, low, entry, stack = pl.pallas_call(
        noise_kernel,
        in_specs=[vmem()] * 4,
        out_specs=[vmem()] * 4,
        out_shape=[
            jax.ShapeDtypeStruct((cadences, cadences), BF16),
            jax.ShapeDtypeStruct((cadences, cadences), BF16),
            jax.ShapeDtypeStruct((96, cadences), BF16),
            jax.ShapeDtypeStruct((96, cadences), BF16),
        ],
        compiler_params=params(16),
        cost_estimate=cost(2 << 30, 2 * MIB),
        name="noise",
    )(later_decay, load_u, feed_w, later_basis)
    fitted, counts, high, low, entry, stack = lax.optimization_barrier(
        (fitted, counts, high, low, entry, stack)
    )

    rows = pl.pallas_call(
        map_kernel,
        in_specs=[vmem()] * 7,
        out_specs=vmem(),
        out_shape=jax.ShapeDtypeStruct((blocks, 16, OWN), F32),
        compiler_params=params(16),
        cost_estimate=cost(1 << 28, 6 * MIB),
        name="map",
    )(fitted, counts, prec, factor, upper, pivot, right)
    rows = lax.all_to_all(rows, "tm", 0, 0, tiled=True)

    carries = pl.pallas_call(
        carry_kernel,
        in_specs=[vmem()] * 3,
        out_specs=vmem(),
        out_shape=jax.ShapeDtypeStruct((blocks, 32, OWN), F32),
        compiler_params=params(16),
        cost_estimate=cost(1 << 24, 3 * MIB),
        name="local_carry",
    )(rows, crossed, decayed)
    carries, later_rows = lax.optimization_barrier((carries, rows))
    carries = lax.all_to_all(carries, "tm", 0, 0, tiled=True)

    part_spec = pl.BlockSpec((WHITEN_CHUNKS, 16, OWN), lambda i: (i, 0, 0))
    tall_spec = pl.BlockSpec((WHITEN_STEP, cadences), lambda i: (i, 0))
    coeffs, local = pl.pallas_call(
        local_kernel,
        grid=(stars // WHITEN_STEP,),
        in_specs=[tall_spec, part_spec, vmem(), vmem(), vmem()],
        out_specs=[pl.BlockSpec((16, WHITEN_STEP), lambda i: (0, i)), tall_spec],
        out_shape=[
            jax.ShapeDtypeStruct((16, stars), F32),
            jax.ShapeDtypeStruct((stars, cadences), F32),
        ],
        compiler_params=params(16),
        cost_estimate=cost(2 * stars * cadences * 1500, 10 * MIB),
        name="local",
    )(marked, later_rows, stack, high, low)
    carries, local = lax.optimization_barrier((carries, local))

    states = pl.pallas_call(
        state_kernel,
        in_specs=[vmem()],
        out_specs=vmem(),
        out_shape=jax.ShapeDtypeStruct((blocks, 16, OWN), F32),
        compiler_params=params(16),
        cost_estimate=cost(1 << 20, MIB),
        name="state",
    )(carries)
    states = lax.all_to_all(states, "tm", 0, 0, tiled=True)

    whitened = pl.pallas_call(
        finish_kernel,
        grid=(stars // WHITEN_STEP,),
        in_specs=[tall_spec, part_spec, vmem(), vmem()],
        out_specs=tall_spec,
        out_shape=jax.ShapeDtypeStruct((stars, cadences), F32),
        compiler_params=params(16),
        cost_estimate=cost(2 * stars * cadences * 100, 9 * MIB),
        name="finish",
    )(local, states, entry, inv_diag[None, :])
    return coeffs.T, whitened


def solution(mesh):
    devices = mesh.devices
    split = Mesh(devices.reshape(devices.shape[0] // 2, 2, devices.shape[1]), ("y", "c", "tm"))
    star = ("y", "c")
    in_specs = (
        P(star, "tm"),
        P(star, "tm"),
        P(star, "tm"),
        P(None, "tm"),
        P(star, None),
        P(),
        P(None, "tm"),
        P(None, "tm"),
        P(None, "tm"),
        P("tm"),
    )
    out_specs = (P(star, None), P(star, "tm"))
    return jax.shard_map(
        per_device, mesh=split, in_specs=in_specs, out_specs=out_specs, check_vma=False
    )
```

```python
import jax
import jax.numpy as jnp
import numpy as np
from jax import lax
from jax.experimental import pallas as pl
from jax.experimental.pallas import tpu as pltpu
from jax.sharding import Mesh, PartitionSpec as P

BASIS_VECTORS = 16
NOISE_TERMS = 16
NEIGH = 64
DIAGONALS = 9
PAIRS = 136
OWN = 128
CUT = 128
STEP = 512
AHEAD = 2
CROSS_STEP = 512
CROSS_CHUNKS = CROSS_STEP // OWN
CHUNKS = STEP // OWN
GRAM_ROWS = PAIRS + 16
CROSS_ROWS = 16 + BASIS_VECTORS * NOISE_TERMS
WHITEN_STEP = 1024
WHITEN_CHUNKS = WHITEN_STEP // OWN

F32 = jnp.float32
BF16 = jnp.bfloat16
MIB = 1 << 20


def split3(x):
    high = x.astype(BF16)
    rest = x - high.astype(F32)
    mid = rest.astype(BF16)
    low = (rest - mid.astype(F32)).astype(BF16)
    return high, mid, low


def left_stack(x):
    high, mid, low = split3(x)
    return jnp.concatenate([high, high, mid, high, mid, low], axis=0)


def right_stack(x):
    high, mid, low = split3(x)
    return jnp.concatenate([high, mid, high, low, mid, high], axis=0)


def dot_nt(a, b):
    return lax.dot_general(a, b, (((1,), (1,)), ((), ())), preferred_element_type=F32)


def dot_tn(a, b):
    return lax.dot_general(a, b, (((0,), (0,)), ((), ())), preferred_element_type=F32)


def dot_nn(a, b):
    return lax.dot_general(a, b, (((1,), (0,)), ((), ())), preferred_element_type=F32)


def masked_sums(x, mask):
    rows = x.shape[0]
    stacked = jnp.concatenate(split3(x), axis=0)
    sums = dot_nn(stacked, mask.astype(F32).astype(BF16))
    return sums[0:rows] + (sums[rows : 2 * rows] + sums[2 * rows : 3 * rows])


def narrow_dots(table_ref, start, x, pieces):
    parts = split3(x)[:pieces]
    sums = [
        dot_nt(table_ref[start : start + 16 * (3 - place), :], part)
        for place, part in enumerate(parts)
    ]
    total = sums[0][32:48]
    for place in range(1, pieces):
        total = total + sums[place][16 * (2 - place) : 16 * (3 - place)]
    mid = sums[0][16:32] + sums[1][0:16]
    return sums[0][0:16] + (mid + total)


def gram_kernel(
    flux_hbm, valid_hbm, quality_hbm, basis_ref, out_ref, flux_ref, valid_ref, quality_ref, table_ref, arrived
):
    wide = DIAGONALS * BASIS_VECTORS
    rights = 3 * wide
    steps = flux_ref.shape[0] // STEP
    pairs = ((flux_hbm, flux_ref), (valid_hbm, valid_ref), (quality_hbm, quality_ref))

    def arrival(which, step):
        source, target = pairs[which]
        stars = pl.ds(step * STEP, STEP)
        return pltpu.make_async_copy(source.at[stars], target.at[stars], arrived.at[which, step])

    for step in range(AHEAD):
        for which in range(3):
            arrival(which, step).start()

    basis = basis_ref[...]
    scaled = basis * (1.0 / 12.0)
    products = []
    for diagonal in range(DIAGONALS):
        turned = basis
        if diagonal:
            turned = jnp.concatenate([basis[diagonal:], basis[:diagonal]], axis=0)
        products.append(scaled * turned)
    for place, piece in enumerate(split3(jnp.concatenate(products, axis=0))):
        table_ref[place * wide : (place + 1) * wide, :] = piece
    for place, piece in enumerate(split3(scaled)):
        table_ref[rights + place * 16 : rights + place * 16 + 16, :] = piece

    for step in range(steps):
        for which in range(3):
            arrival(which, step).wait()
            if step + AHEAD < steps:
                arrival(which, step + AHEAD).start()
        stars = slice(step * STEP, (step + 1) * STEP)
        quality = quality_ref[stars, :]
        twelfths = jnp.where(
            quality == 0, 12.0, jnp.where(quality == 1, 6.0, jnp.where(quality == 2, 4.0, 3.0))
        )
        weight = jnp.where(valid_ref[stars, :] != 0, twelfths, 0.0)
        grams = dot_nt(table_ref[0:rights, :], weight.astype(BF16))
        gram = grams[0:PAIRS] + (grams[wide : wide + PAIRS] + grams[2 * wide : 2 * wide + PAIRS])
        right = narrow_dots(table_ref, rights, weight * flux_ref[stars, :], 3)
        for chunk in range(CHUNKS):
            lanes = slice(chunk * OWN, (chunk + 1) * OWN)
            out_ref[step * CHUNKS + chunk, 0:PAIRS, :] = gram[:, lanes]
            out_ref[step * CHUNKS + chunk, PAIRS:GRAM_ROWS, :] = right[:, lanes]


def cross_kernel(
    flux_ref, valid_ref, basis_ref, decay_ref, feed_ref, out_ref, decayed_ref, marked_ref, table_ref
):
    cross = BASIS_VECTORS * NOISE_TERMS
    feeds = 2 * cross

    @pl.when(pl.program_id(0) == 0)
    def _():
        log_decay = jnp.log(decay_ref[...])
        count = log_decay.shape[1]
        rows = lax.broadcasted_iota(jnp.int32, (count, count), 0)
        columns = lax.broadcasted_iota(jnp.int32, (count, count), 1)
        suffix = masked_sums(log_decay, rows > columns)
        feed = jnp.exp(suffix) * feed_ref[...]
        whole = jnp.exp(suffix[:, 0:1] + log_decay[:, 0:1])
        decayed_ref[...] = jnp.broadcast_to(whole, (NOISE_TERMS, OWN))
        for k in range(BASIS_VECTORS):
            product = basis_ref[k : k + 1, :] * feed
            for place, piece in enumerate(split3(product)[:2]):
                first = place * cross + k * 16
                table_ref[first : first + 16, :] = piece
        for place, piece in enumerate(split3(feed)):
            table_ref[feeds + place * 16 : feeds + place * 16 + 16, :] = piece

    usable = valid_ref[...] != 0
    flux = flux_ref[...]
    marked_ref[...] = jnp.where(usable, flux, jnp.nan)
    sums = dot_nt(table_ref[0:feeds, :], jnp.where(usable, 1.0, 0.0).astype(BF16))
    crossed = sums[0:cross] + sums[cross : 2 * cross]
    plain = narrow_dots(table_ref, feeds, jnp.where(usable, flux, 0.0), 2)
    for chunk in range(CROSS_CHUNKS):
        lanes = slice(chunk * OWN, (chunk + 1) * OWN)
        out_ref[chunk, 0:16, :] = plain[:, lanes]
        out_ref[chunk, 16:CROSS_ROWS, :] = crossed[:, lanes]


def count_kernel(code_ref, low_ref, out_ref):
    entries = 8 * NEIGH
    row_code = lax.broadcasted_iota(jnp.int32, (128 * 8, entries), 0)
    low_code = lax.broadcasted_iota(jnp.int32, (128, entries), 0)

    def one_half(group):
        code = code_ref[pl.ds(group, 1), :]
        low = low_ref[pl.ds(group, 1), :]
        highs = jnp.where(row_code == code, 1.0, 0.0).astype(BF16)
        lows = jnp.where(low_code == low, 1.0, 0.0).astype(BF16)
        return dot_nt(highs, lows).reshape(128, 8, 128)

    def one(step, ignored):
        both = jnp.concatenate([one_half(2 * step), one_half(2 * step + 1)], axis=1)
        out_ref[:, pl.ds(pl.multiple_of(step * 16, 16), 16), :] = both.astype(BF16)
        return ignored

    lax.fori_loop(0, OWN // 16, one, 0)


def noise_kernel(
    decay_ref, load_ref, feed_ref, basis_ref, high_ref, low_ref, entry_ref, stack_ref
):
    log_decay = jnp.log(decay_ref[...])
    load = load_ref[...]
    feed = feed_ref[...]
    count = log_decay.shape[1]
    rows = lax.broadcasted_iota(jnp.int32, (count, count), 0)
    columns = lax.broadcasted_iota(jnp.int32, (count, count), 1)
    together = (rows // CUT) == (columns // CUT)
    before = masked_sums(log_decay, together & (rows < columns))
    tail = masked_sums(log_decay, together & (rows > columns))
    through = before + log_decay
    cuts = count // CUT
    totals = [through[:, (cut + 1) * CUT - 1 : (cut + 1) * CUT] for cut in range(cuts)]
    lower = lax.broadcasted_iota(jnp.int32, (CUT, CUT), 0) < lax.broadcasted_iota(
        jnp.int32, (CUT, CUT), 1
    )
    high_ref[...] = jnp.zeros_like(high_ref)
    low_ref[...] = jnp.zeros_like(low_ref)

    def keep(u, t, block):
        high = block.astype(BF16)
        span = (slice(u * CUT, (u + 1) * CUT), slice(t * CUT, (t + 1) * CUT))
        high_ref[span] = high
        low_ref[span] = (block - high.astype(F32)).astype(BF16)

    passed = jnp.zeros((NOISE_TERMS, 1), F32)
    entries = []
    for t in range(cuts):
        lanes = slice(t * CUT, (t + 1) * CUT)
        middle = through[:, t * CUT + CUT // 2 - 1 : t * CUT + CUT // 2]
        near_left = feed[:, lanes] * jnp.exp(middle - through[:, lanes])
        near_right = load[:, lanes] * jnp.exp(before[:, lanes] - middle)
        near = dot_tn(left_stack(near_left), right_stack(near_right))
        keep(t, t, jnp.where(lower, near, 0.0))
        far_right = right_stack(load[:, lanes] * jnp.exp(before[:, lanes]))
        between = jnp.zeros((NOISE_TERMS, 1), F32)
        for u in range(t - 1, -1, -1):
            span = slice(u * CUT, (u + 1) * CUT)
            far_left = left_stack(feed[:, span] * jnp.exp(tail[:, span] + between))
            keep(u, t, dot_tn(far_left, far_right))
            between = between + totals[u]
        entries.append(load[:, lanes] * jnp.exp(before[:, lanes] + passed))
        passed = passed + totals[t]
    entry_ref[...] = right_stack(jnp.concatenate(entries, axis=1))
    stack_ref[...] = right_stack(basis_ref[...])


def row_of_pair(i, j):
    apart = (j - i) % BASIS_VECTORS
    if apart < 8 or (apart == 8 and i < 8):
        return apart * BASIS_VECTORS + i
    return ((i - j) % BASIS_VECTORS) * BASIS_VECTORS + j


def eliminate(columns, vector):
    order = BASIS_VECTORS
    columns = list(columns)
    rows = lax.broadcasted_iota(jnp.int32, columns[0].shape, 0)
    scaled, pivots = [], []
    for k in range(order):
        inverse = 1.0 / columns[k][k : k + 1, :]
        factor = jnp.where(rows > k, columns[k] * inverse, 0.0)
        for j in range(k + 1, order):
            columns[j] = columns[j] - factor * columns[j][k : k + 1, :]
        scaled.append(factor)
        pivots.append(inverse)
        if vector is not None:
            vector = vector - factor * vector[k : k + 1, :]
    return scaled, pivots, vector, columns


def back_substitute(vector, uppers, pivots):
    rows = lax.broadcasted_iota(jnp.int32, vector.shape, 0)
    solved = jnp.zeros_like(vector)
    for k in range(BASIS_VECTORS - 1, -1, -1):
        value = vector[k : k + 1, :] * pivots[k]
        vector = vector - uppers[k] * value
        solved = jnp.where(rows == k, value, solved)
    return solved


def solve_kernel(parts_ref, prec_ref, fitted_ref, kept_ref, sums_ref, matrix_ref):
    total = parts_ref[0]
    for part in range(1, parts_ref.shape[0]):
        total = total + parts_ref[part]
    sums_ref[...] = total
    right = total[PAIRS : PAIRS + 16]
    kept_ref[33] = right
    order = BASIS_VECTORS
    for j in range(order):
        for i in range(order):
            row = row_of_pair(i, j)
            matrix_ref[j * order + i : j * order + i + 1, :] = sums_ref[row : row + 1, :]
    rows = lax.broadcasted_iota(jnp.int32, right.shape, 0)
    plain = [matrix_ref[j * order : (j + 1) * order, :] for j in range(order)]
    prec = prec_ref[...]
    ridged = [jnp.where(rows == j, plain[j] + 0.1, plain[j]) for j in range(order)]
    ignored, pivots, reduced, uppers = eliminate(ridged, right)
    fitted = back_substitute(reduced, uppers, pivots)
    for peer in range(fitted_ref.shape[0]):
        fitted_ref[peer] = fitted
    weighted = [jnp.where(rows == j, plain[j] + prec, plain[j]) for j in range(order)]
    factors, pivots, ignored, uppers = eliminate(weighted, None)
    for k in range(order):
        kept_ref[k] = factors[k]
        kept_ref[16 + k] = uppers[k]
        kept_ref[32, k : k + 1, :] = pivots[k]


def map_kernel(near_ref, far_ref, counts_ref, prec_ref, kept_ref, out_ref):
    half = near_ref.shape[0]
    prior = jnp.zeros((48, OWN), F32)
    for spot in range(0, 2 * half, 2):
        table_ref, place = (near_ref, spot) if spot < half else (far_ref, spot - half)
        wide = jnp.concatenate([table_ref[place], table_ref[place + 1]], axis=1)
        listed = jnp.concatenate([counts_ref[spot], counts_ref[spot + 1]], axis=1)
        prior = prior + dot_nt(jnp.concatenate(split3(wide), axis=0), listed)
    prior_mean = (prior[0:16] + (prior[16:32] + prior[32:48])) * (1.0 / NEIGH)
    vector = kept_ref[33] + prec_ref[...] * prior_mean
    for k in range(BASIS_VECTORS):
        vector = vector - kept_ref[k] * vector[k : k + 1, :]
    uppers = [kept_ref[16 + k] for k in range(BASIS_VECTORS)]
    pivots = [kept_ref[32, k : k + 1, :] for k in range(BASIS_VECTORS)]
    coeffs = back_substitute(vector, uppers, pivots)
    for peer in range(out_ref.shape[0]):
        out_ref[peer] = coeffs


def carry_kernel(rows_ref, crossed_ref, decayed_ref, out_ref):
    for owner in range(rows_ref.shape[0]):
        coeffs = rows_ref[owner]
        carry = crossed_ref[owner, 0:16, :]
        for k in range(BASIS_VECTORS):
            first = 16 + 16 * k
            carry = carry - coeffs[k : k + 1, :] * crossed_ref[owner, first : first + 16, :]
        out_ref[owner, 0:16, :] = carry
        out_ref[owner, 16:32, :] = decayed_ref[...]


def state_kernel(carry_ref, out_ref):
    state = jnp.zeros((NOISE_TERMS, OWN), F32)
    for block in range(carry_ref.shape[0]):
        out_ref[block] = state
        state = state * carry_ref[block, 16:32, :] + carry_ref[block, 0:16, :]


def whiten_kernel(
    marked_ref, rows_ref, states_ref, stack_ref, entry_ref, high_ref, low_ref, scale_ref, coeffs_ref, out_ref
):
    coeffs = jnp.concatenate([rows_ref[chunk] for chunk in range(WHITEN_CHUNKS)], axis=1)
    states = jnp.concatenate([states_ref[chunk] for chunk in range(WHITEN_CHUNKS)], axis=1)
    coeffs_ref[...] = coeffs
    trend = dot_tn(left_stack(coeffs), stack_ref[...])
    first = pl.multiple_of(pl.program_id(0) * WHITEN_STEP, WHITEN_STEP)
    marked = marked_ref[pl.ds(first, WHITEN_STEP), :]
    residual = jnp.where(marked == marked, marked - trend, 0.0)
    incoming = dot_tn(left_stack(states), entry_ref[...])
    high = residual.astype(BF16)
    low = (residual - high.astype(F32)).astype(BF16)
    count = residual.shape[1]
    for first in range(0, count, 256):
        lanes = slice(first, first + 256)
        upto = slice(0, first + 256)
        local = dot_nn(low[:, upto], high_ref[upto, lanes]) + dot_nn(high[:, upto], low_ref[upto, lanes])
        local = local + dot_nn(high[:, upto], high_ref[upto, lanes])
        out_ref[:, lanes] = (residual[:, lanes] - local - incoming[:, lanes]) * scale_ref[:, lanes]


def vmem():
    return pl.BlockSpec(memory_space=pltpu.VMEM)


def params(mib):
    return pltpu.CompilerParams(vmem_limit_bytes=mib * MIB)


def cost(flops, bytes_accessed):
    return pl.CostEstimate(flops=flops, bytes_accessed=bytes_accessed, transcendentals=0)


def per_device(
    flux, valid, quality, basis, neighbours, prior_prec, decay, load_u, feed_w, inv_diag
):
    stars, cadences = flux.shape
    blocks = stars // OWN
    place = lax.axis_index("tm")
    prec = jnp.broadcast_to(prior_prec[:, None], (BASIS_VECTORS, OWN))

    listed = lax.dynamic_slice_in_dim(neighbours, place * OWN, OWN, 0).reshape(blocks, -1)
    low_bits = listed & 127
    owner = listed >> 7
    spot = (owner & 15) + 16 * (owner >> 5) + 64 * (((owner >> 4) & 1) ^ lax.axis_index("c"))
    code = spot * 8 + lax.broadcasted_iota(jnp.int32, listed.shape, 1) // NEIGH

    in_hbm = pl.BlockSpec(memory_space=pl.ANY)
    parts = pl.pallas_call(
        gram_kernel,
        in_specs=[in_hbm] * 3 + [vmem()],
        out_specs=vmem(),
        out_shape=jax.ShapeDtypeStruct((blocks, GRAM_ROWS, OWN), F32),
        scratch_shapes=[
            pltpu.VMEM((stars, cadences), F32),
            pltpu.VMEM((stars, cadences), jnp.int32),
            pltpu.VMEM((stars, cadences), jnp.int32),
            pltpu.VMEM((480, cadences), BF16),
            pltpu.SemaphoreType.DMA((3, stars // STEP)),
        ],
        compiler_params=params(58),
        cost_estimate=cost(2 * stars * cadences * 600, 14 * MIB),
        name="gram",
    )(flux, valid, quality, basis)

    parts, later_basis, later_decay = lax.optimization_barrier((parts, basis, decay))
    cross_spec = pl.BlockSpec((CROSS_STEP, cadences), lambda i: (i, 0))
    table_spec = pl.BlockSpec((16, cadences), lambda i: (0, 0))
    crossed, decayed, marked = pl.pallas_call(
        cross_kernel,
        grid=(stars // CROSS_STEP,),
        in_specs=[cross_spec, cross_spec, table_spec, table_spec, table_spec],
        out_specs=[
            pl.BlockSpec((CROSS_CHUNKS, CROSS_ROWS, OWN), lambda i: (i, 0, 0)),
            pl.BlockSpec((NOISE_TERMS, OWN), lambda i: (0, 0)),
            cross_spec,
        ],
        out_shape=[
            jax.ShapeDtypeStruct((blocks, CROSS_ROWS, OWN), F32),
            jax.ShapeDtypeStruct((NOISE_TERMS, OWN), F32),
            jax.ShapeDtypeStruct((stars, cadences), F32),
        ],
        scratch_shapes=[pltpu.VMEM((560, cadences), BF16)],
        compiler_params=params(58),
        cost_estimate=cost(2 * stars * cadences * 800, 16 * MIB),
        name="cross",
    )(flux, valid, later_basis, later_decay, feed_w)
    parts = lax.all_to_all(parts, "tm", 0, 0, tiled=True)
    parts, crossed, decayed, marked = lax.optimization_barrier((parts, crossed, decayed, marked))

    nearby = ("y", "tm")
    copies = jax.ShapeDtypeStruct((lax.axis_size(nearby), 16, OWN), F32)
    fitted, kept = pl.pallas_call(
        solve_kernel,
        in_specs=[vmem()] * 2,
        out_specs=[vmem()] * 2,
        out_shape=[copies, jax.ShapeDtypeStruct((34, 16, OWN), F32)],
        scratch_shapes=[pltpu.VMEM((GRAM_ROWS, OWN), F32), pltpu.VMEM((256, OWN), F32)],
        compiler_params=params(16),
        cost_estimate=cost(1 << 20, 2 * MIB),
        name="solve",
    )(parts, prec)

    fitted, later_code, later_low = lax.optimization_barrier((fitted, code, low_bits))
    near = lax.all_to_all(fitted, nearby, 0, 0, tiled=True)
    counts = pl.pallas_call(
        count_kernel,
        in_specs=[vmem(), vmem()],
        out_specs=vmem(),
        out_shape=jax.ShapeDtypeStruct((128, OWN, 128), BF16),
        compiler_params=params(16),
        cost_estimate=cost(4 << 30, 4 * MIB),
        name="count",
    )(later_code, later_low)
    near, counts = lax.optimization_barrier((near, counts))
    far = lax.ppermute(near, "c", [(0, 1), (1, 0)])

    rows = pl.pallas_call(
        map_kernel,
        in_specs=[vmem()] * 5,
        out_specs=vmem(),
        out_shape=jax.ShapeDtypeStruct((blocks, 16, OWN), F32),
        compiler_params=params(16),
        cost_estimate=cost(1 << 28, 6 * MIB),
        name="map",
    )(near, far, counts, prec, kept)
    rows = lax.all_to_all(rows, "tm", 0, 0, tiled=True)

    carries = pl.pallas_call(
        carry_kernel,
        in_specs=[vmem()] * 3,
        out_specs=vmem(),
        out_shape=jax.ShapeDtypeStruct((blocks, 32, OWN), F32),
        compiler_params=params(16),
        cost_estimate=cost(1 << 24, 3 * MIB),
        name="local_carry",
    )(rows, crossed, decayed)
    carries = lax.all_to_all(carries, "tm", 0, 0, tiled=True)
    states = pl.pallas_call(
        state_kernel,
        in_specs=[vmem()],
        out_specs=vmem(),
        out_shape=jax.ShapeDtypeStruct((blocks, 16, OWN), F32),
        compiler_params=params(16),
        cost_estimate=cost(1 << 20, MIB),
        name="state",
    )(carries)
    states = lax.all_to_all(states, "tm", 0, 0, tiled=True)

    states, last_decay, last_basis = lax.optimization_barrier((states, decay, basis))
    high, low, entry, stack = pl.pallas_call(
        noise_kernel,
        in_specs=[vmem()] * 4,
        out_specs=[vmem()] * 4,
        out_shape=[
            jax.ShapeDtypeStruct((cadences, cadences), BF16),
            jax.ShapeDtypeStruct((cadences, cadences), BF16),
            jax.ShapeDtypeStruct((96, cadences), BF16),
            jax.ShapeDtypeStruct((96, cadences), BF16),
        ],
        compiler_params=params(16),
        cost_estimate=cost(2 << 30, 2 * MIB),
        name="noise",
    )(last_decay, load_u, feed_w, last_basis)
    part_spec = pl.BlockSpec((WHITEN_CHUNKS, 16, OWN), lambda i: (i, 0, 0))
    coeffs, whitened = pl.pallas_call(
        whiten_kernel,
        grid=(stars // WHITEN_STEP,),
        in_specs=[vmem(), part_spec, part_spec] + [vmem()] * 5,
        out_specs=[
            pl.BlockSpec((16, WHITEN_STEP), lambda i: (0, i)),
            pl.BlockSpec((WHITEN_STEP, cadences), lambda i: (i, 0)),
        ],
        out_shape=[
            jax.ShapeDtypeStruct((16, stars), F32),
            jax.ShapeDtypeStruct((stars, cadences), F32),
        ],
        compiler_params=params(32),
        cost_estimate=cost(2 * stars * cadences * 1700, 14 * MIB),
        name="whiten",
    )(marked, rows, states, stack, entry, high, low, inv_diag[None, :])
    return coeffs.T, whitened


def solution(mesh):
    devices = mesh.devices
    split = Mesh(devices.reshape(devices.shape[0] // 2, 2, devices.shape[1]), ("y", "c", "tm"))
    star = ("y", "c")
    in_specs = (
        P(star, "tm"),
        P(star, "tm"),
        P(star, "tm"),
        P(None, "tm"),
        P(star, None),
        P(),
        P(None, "tm"),
        P(None, "tm"),
        P(None, "tm"),
        P("tm"),
    )
    out_specs = (P(star, None), P(star, "tm"))
    return jax.shard_map(
        per_device, mesh=split, in_specs=in_specs, out_specs=out_specs, check_vma=False
    )
```

```python
import jax
import jax.numpy as jnp
import numpy as np
from jax import lax
from jax.experimental import pallas as pl
from jax.experimental.pallas import tpu as pltpu
from jax.sharding import Mesh, PartitionSpec as P

BASIS_VECTORS = 16
NOISE_TERMS = 16
NEIGH = 64
DIAGONALS = 9
PAIRS = 136
OWN = 128
CUT = 128
STEP = 512
AHEAD = 2
CROSS_STEP = 512
CROSS_CHUNKS = CROSS_STEP // OWN
CHUNKS = STEP // OWN
GRAM_ROWS = PAIRS + 16
CROSS_ROWS = 16 + BASIS_VECTORS * NOISE_TERMS
WHITEN_STEP = 1024
WHITEN_CHUNKS = WHITEN_STEP // OWN

F32 = jnp.float32
BF16 = jnp.bfloat16
MIB = 1 << 20


def split3(x):
    high = x.astype(BF16)
    rest = x - high.astype(F32)
    mid = rest.astype(BF16)
    low = (rest - mid.astype(F32)).astype(BF16)
    return high, mid, low


def left_stack(x):
    high, mid, low = split3(x)
    return jnp.concatenate([high, high, mid, high, mid, low], axis=0)


def right_stack(x):
    high, mid, low = split3(x)
    return jnp.concatenate([high, mid, high, low, mid, high], axis=0)


def dot_nt(a, b):
    return lax.dot_general(a, b, (((1,), (1,)), ((), ())), preferred_element_type=F32)


def dot_tn(a, b):
    return lax.dot_general(a, b, (((0,), (0,)), ((), ())), preferred_element_type=F32)


def dot_nn(a, b):
    return lax.dot_general(a, b, (((1,), (0,)), ((), ())), preferred_element_type=F32)


def masked_sums(x, mask):
    rows = x.shape[0]
    stacked = jnp.concatenate(split3(x), axis=0)
    sums = dot_nn(stacked, mask.astype(F32).astype(BF16))
    return sums[0:rows] + (sums[rows : 2 * rows] + sums[2 * rows : 3 * rows])


def narrow_dots(table_ref, start, x, pieces):
    parts = split3(x)[:pieces]
    sums = [
        dot_nt(table_ref[start : start + 16 * (3 - place), :], part)
        for place, part in enumerate(parts)
    ]
    total = sums[0][32:48]
    for place in range(1, pieces):
        total = total + sums[place][16 * (2 - place) : 16 * (3 - place)]
    mid = sums[0][16:32] + sums[1][0:16]
    return sums[0][0:16] + (mid + total)


def gram_kernel(
    flux_hbm, valid_hbm, quality_hbm, basis_ref, out_ref, flux_ref, valid_ref, quality_ref, table_ref, arrived
):
    wide = DIAGONALS * BASIS_VECTORS
    rights = 3 * wide
    steps = flux_ref.shape[0] // STEP
    pairs = ((flux_hbm, flux_ref), (valid_hbm, valid_ref), (quality_hbm, quality_ref))

    def arrival(which, step):
        source, target = pairs[which]
        stars = pl.ds(step * STEP, STEP)
        return pltpu.make_async_copy(source.at[stars], target.at[stars], arrived.at[which, step])

    for step in range(AHEAD):
        for which in range(3):
            arrival(which, step).start()

    basis = basis_ref[...]
    scaled = basis * (1.0 / 12.0)
    products = []
    for diagonal in range(DIAGONALS):
        turned = basis
        if diagonal:
            turned = jnp.concatenate([basis[diagonal:], basis[:diagonal]], axis=0)
        products.append(scaled * turned)
    for place, piece in enumerate(split3(jnp.concatenate(products, axis=0))):
        table_ref[place * wide : (place + 1) * wide, :] = piece
    for place, piece in enumerate(split3(scaled)):
        table_ref[rights + place * 16 : rights + place * 16 + 16, :] = piece

    for step in range(steps):
        for which in range(3):
            arrival(which, step).wait()
            if step + AHEAD < steps:
                arrival(which, step + AHEAD).start()
        stars = slice(step * STEP, (step + 1) * STEP)
        quality = quality_ref[stars, :]
        twelfths = jnp.where(
            quality == 0, 12.0, jnp.where(quality == 1, 6.0, jnp.where(quality == 2, 4.0, 3.0))
        )
        weight = jnp.where(valid_ref[stars, :] != 0, twelfths, 0.0)
        grams = dot_nt(table_ref[0:rights, :], weight.astype(BF16))
        gram = grams[0:PAIRS] + (grams[wide : wide + PAIRS] + grams[2 * wide : 2 * wide + PAIRS])
        right = narrow_dots(table_ref, rights, weight * flux_ref[stars, :], 3)
        for chunk in range(CHUNKS):
            lanes = slice(chunk * OWN, (chunk + 1) * OWN)
            out_ref[step * CHUNKS + chunk, 0:PAIRS, :] = gram[:, lanes]
            out_ref[step * CHUNKS + chunk, PAIRS:GRAM_ROWS, :] = right[:, lanes]


def cross_kernel(
    flux_ref, valid_ref, basis_ref, decay_ref, feed_ref, out_ref, decayed_ref, table_ref
):
    cross = BASIS_VECTORS * NOISE_TERMS
    feeds = 2 * cross

    @pl.when(pl.program_id(0) == 0)
    def _():
        log_decay = jnp.log(decay_ref[...])
        count = log_decay.shape[1]
        rows = lax.broadcasted_iota(jnp.int32, (count, count), 0)
        columns = lax.broadcasted_iota(jnp.int32, (count, count), 1)
        suffix = masked_sums(log_decay, rows > columns)
        feed = jnp.exp(suffix) * feed_ref[...]
        whole = jnp.exp(suffix[:, 0:1] + log_decay[:, 0:1])
        decayed_ref[...] = jnp.broadcast_to(whole, (NOISE_TERMS, OWN))
        for k in range(BASIS_VECTORS):
            product = basis_ref[k : k + 1, :] * feed
            for place, piece in enumerate(split3(product)[:2]):
                first = place * cross + k * 16
                table_ref[first : first + 16, :] = piece
        for place, piece in enumerate(split3(feed)):
            table_ref[feeds + place * 16 : feeds + place * 16 + 16, :] = piece

    usable = valid_ref[...] != 0
    flux = flux_ref[...]
    sums = dot_nt(table_ref[0:feeds, :], jnp.where(usable, 1.0, 0.0).astype(BF16))
    crossed = sums[0:cross] + sums[cross : 2 * cross]
    plain = narrow_dots(table_ref, feeds, jnp.where(usable, flux, 0.0), 2)
    for chunk in range(CROSS_CHUNKS):
        lanes = slice(chunk * OWN, (chunk + 1) * OWN)
        out_ref[chunk, 0:16, :] = plain[:, lanes]
        out_ref[chunk, 16:CROSS_ROWS, :] = crossed[:, lanes]


def count_kernel(code_ref, low_ref, near_ref, far_ref):
    entries = 8 * NEIGH
    half, lows_all = near_ref.shape[0], near_ref.shape[2]
    row_code = lax.broadcasted_iota(jnp.int32, (2 * half * 8, entries), 0)
    low_code = lax.broadcasted_iota(jnp.int32, (lows_all, entries), 0)

    def one_half(group):
        code = code_ref[pl.ds(group, 1), :]
        low = low_ref[pl.ds(group, 1), :]
        highs = jnp.where(row_code == code, 1.0, 0.0).astype(BF16)
        lows = jnp.where(low_code == low, 1.0, 0.0).astype(BF16)
        return dot_nt(highs, lows).reshape(2 * half, 8, lows_all)

    def one(step, ignored):
        both = jnp.concatenate([one_half(2 * step), one_half(2 * step + 1)], axis=1).astype(BF16)
        span = pl.ds(pl.multiple_of(step * 16, 16), 16)
        near_ref[:, span, :] = both[:half]
        far_ref[:, span, :] = both[half:]
        return ignored

    lax.fori_loop(0, OWN // 16, one, 0)


def noise_kernel(
    decay_ref, load_ref, feed_ref, basis_ref, high_ref, low_ref, entry_ref, stack_ref
):
    log_decay = jnp.log(decay_ref[...])
    load = load_ref[...]
    feed = feed_ref[...]
    count = log_decay.shape[1]
    rows = lax.broadcasted_iota(jnp.int32, (count, count), 0)
    columns = lax.broadcasted_iota(jnp.int32, (count, count), 1)
    together = (rows // CUT) == (columns // CUT)
    before = masked_sums(log_decay, together & (rows < columns))
    tail = masked_sums(log_decay, together & (rows > columns))
    through = before + log_decay
    cuts = count // CUT
    totals = [through[:, (cut + 1) * CUT - 1 : (cut + 1) * CUT] for cut in range(cuts)]
    lower = lax.broadcasted_iota(jnp.int32, (CUT, CUT), 0) < lax.broadcasted_iota(
        jnp.int32, (CUT, CUT), 1
    )
    high_ref[...] = jnp.zeros_like(high_ref)
    low_ref[...] = jnp.zeros_like(low_ref)

    def keep(u, t, block):
        high = block.astype(BF16)
        span = (slice(u * CUT, (u + 1) * CUT), slice(t * CUT, (t + 1) * CUT))
        high_ref[span] = high
        low_ref[span] = (block - high.astype(F32)).astype(BF16)

    passed = jnp.zeros((NOISE_TERMS, 1), F32)
    entries = []
    for t in range(cuts):
        lanes = slice(t * CUT, (t + 1) * CUT)
        middle = through[:, t * CUT + CUT // 2 - 1 : t * CUT + CUT // 2]
        near_left = feed[:, lanes] * jnp.exp(middle - through[:, lanes])
        near_right = load[:, lanes] * jnp.exp(before[:, lanes] - middle)
        near = dot_tn(left_stack(near_left), right_stack(near_right))
        keep(t, t, jnp.where(lower, near, 0.0))
        far_right = right_stack(load[:, lanes] * jnp.exp(before[:, lanes]))
        between = jnp.zeros((NOISE_TERMS, 1), F32)
        for u in range(t - 1, -1, -1):
            span = slice(u * CUT, (u + 1) * CUT)
            far_left = left_stack(feed[:, span] * jnp.exp(tail[:, span] + between))
            keep(u, t, dot_tn(far_left, far_right))
            between = between + totals[u]
        entries.append(load[:, lanes] * jnp.exp(before[:, lanes] + passed))
        passed = passed + totals[t]
    entry_ref[...] = right_stack(jnp.concatenate(entries, axis=1))
    stack_ref[...] = right_stack(basis_ref[...])


def row_of_pair(i, j):
    apart = (j - i) % BASIS_VECTORS
    if apart < 8 or (apart == 8 and i < 8):
        return apart * BASIS_VECTORS + i
    return ((i - j) % BASIS_VECTORS) * BASIS_VECTORS + j


def eliminate(columns, vector):
    order = BASIS_VECTORS
    columns = list(columns)
    rows = lax.broadcasted_iota(jnp.int32, columns[0].shape, 0)
    scaled, pivots = [], []
    for k in range(order):
        inverse = 1.0 / columns[k][k : k + 1, :]
        factor = jnp.where(rows > k, columns[k] * inverse, 0.0)
        for j in range(k + 1, order):
            columns[j] = columns[j] - factor * columns[j][k : k + 1, :]
        scaled.append(factor)
        pivots.append(inverse)
        if vector is not None:
            vector = vector - factor * vector[k : k + 1, :]
    return scaled, pivots, vector, columns


def back_substitute(vector, uppers, pivots):
    rows = lax.broadcasted_iota(jnp.int32, vector.shape, 0)
    solved = jnp.zeros_like(vector)
    for k in range(BASIS_VECTORS - 1, -1, -1):
        value = vector[k : k + 1, :] * pivots[k]
        vector = vector - uppers[k] * value
        solved = jnp.where(rows == k, value, solved)
    return solved


def solve_kernel(parts_ref, prec_ref, fitted_ref, kept_ref, sums_ref, matrix_ref):
    total = parts_ref[0]
    for part in range(1, parts_ref.shape[0]):
        total = total + parts_ref[part]
    sums_ref[...] = total
    right = total[PAIRS : PAIRS + 16]
    kept_ref[33] = right
    order = BASIS_VECTORS
    for j in range(order):
        for i in range(order):
            row = row_of_pair(i, j)
            matrix_ref[j * order + i : j * order + i + 1, :] = sums_ref[row : row + 1, :]
    rows = lax.broadcasted_iota(jnp.int32, right.shape, 0)
    plain = [matrix_ref[j * order : (j + 1) * order, :] for j in range(order)]
    prec = prec_ref[...]
    ridged = [jnp.where(rows == j, plain[j] + 0.1, plain[j]) for j in range(order)]
    ignored, pivots, reduced, uppers = eliminate(ridged, right)
    fitted = back_substitute(reduced, uppers, pivots)
    for peer in range(fitted_ref.shape[0]):
        fitted_ref[peer] = fitted
    weighted = [jnp.where(rows == j, plain[j] + prec, plain[j]) for j in range(order)]
    factors, pivots, ignored, uppers = eliminate(weighted, None)
    for k in range(order):
        kept_ref[k] = factors[k]
        kept_ref[16 + k] = uppers[k]
        kept_ref[32, k : k + 1, :] = pivots[k]


def listed_sums(table_ref, counts_ref):
    sums = jnp.zeros((48, OWN), F32)
    for place in range(0, table_ref.shape[0], 2):
        wide = jnp.concatenate([table_ref[place], table_ref[place + 1]], axis=1)
        sums = sums + dot_nt(jnp.concatenate(split3(wide), axis=0), counts_ref[place // 2])
    return sums


def near_kernel(near_ref, counts_ref, out_ref):
    out_ref[...] = listed_sums(near_ref, counts_ref)


def map_kernel(begun_ref, far_ref, counts_ref, prec_ref, kept_ref, out_ref):
    prior = begun_ref[...] + listed_sums(far_ref, counts_ref)
    prior_mean = (prior[0:16] + (prior[16:32] + prior[32:48])) * (1.0 / NEIGH)
    vector = kept_ref[33] + prec_ref[...] * prior_mean
    for k in range(BASIS_VECTORS):
        vector = vector - kept_ref[k] * vector[k : k + 1, :]
    uppers = [kept_ref[16 + k] for k in range(BASIS_VECTORS)]
    pivots = [kept_ref[32, k : k + 1, :] for k in range(BASIS_VECTORS)]
    coeffs = back_substitute(vector, uppers, pivots)
    for peer in range(out_ref.shape[0]):
        out_ref[peer] = coeffs


def carry_kernel(rows_ref, crossed_ref, decayed_ref, out_ref):
    for owner in range(rows_ref.shape[0]):
        coeffs = rows_ref[owner]
        carry = crossed_ref[owner, 0:16, :]
        for k in range(BASIS_VECTORS):
            first = 16 + 16 * k
            carry = carry - coeffs[k : k + 1, :] * crossed_ref[owner, first : first + 16, :]
        out_ref[owner, 0:16, :] = carry
        out_ref[owner, 16:32, :] = decayed_ref[...]


def state_kernel(carry_ref, out_ref):
    state = jnp.zeros((NOISE_TERMS, OWN), F32)
    for block in range(carry_ref.shape[0]):
        out_ref[block] = state
        state = state * carry_ref[block, 16:32, :] + carry_ref[block, 0:16, :]


def whiten_kernel(
    flux_ref, valid_ref, rows_ref, states_ref, stack_ref, entry_ref, high_ref, low_ref, scale_ref, coeffs_ref, out_ref
):
    coeffs = jnp.concatenate([rows_ref[chunk] for chunk in range(WHITEN_CHUNKS)], axis=1)
    states = jnp.concatenate([states_ref[chunk] for chunk in range(WHITEN_CHUNKS)], axis=1)
    coeffs_ref[...] = coeffs
    trend = dot_tn(left_stack(coeffs), stack_ref[...])
    first = pl.multiple_of(pl.program_id(0) * WHITEN_STEP, WHITEN_STEP)
    stars = pl.ds(first, WHITEN_STEP)
    residual = jnp.where(valid_ref[stars, :] != 0, flux_ref[stars, :] - trend, 0.0)
    incoming = dot_tn(left_stack(states), entry_ref[...])
    high = residual.astype(BF16)
    low = (residual - high.astype(F32)).astype(BF16)
    count = residual.shape[1]
    for first in range(0, count, 256):
        lanes = slice(first, first + 256)
        upto = slice(0, first + 256)
        local = dot_nn(low[:, upto], high_ref[upto, lanes]) + dot_nn(high[:, upto], low_ref[upto, lanes])
        local = local + dot_nn(high[:, upto], high_ref[upto, lanes])
        out_ref[:, lanes] = (residual[:, lanes] - local - incoming[:, lanes]) * scale_ref[:, lanes]


def vmem():
    return pl.BlockSpec(memory_space=pltpu.VMEM)


def params(mib):
    return pltpu.CompilerParams(vmem_limit_bytes=mib * MIB)


def cost(flops, bytes_accessed):
    return pl.CostEstimate(flops=flops, bytes_accessed=bytes_accessed, transcendentals=0)


def per_device(
    flux, valid, quality, basis, neighbours, prior_prec, decay, load_u, feed_w, inv_diag
):
    stars, cadences = flux.shape
    blocks = stars // OWN
    place = lax.axis_index("tm")
    prec = jnp.broadcast_to(prior_prec[:, None], (BASIS_VECTORS, OWN))

    in_hbm = pl.BlockSpec(memory_space=pl.ANY)
    parts = pl.pallas_call(
        gram_kernel,
        in_specs=[in_hbm] * 3 + [vmem()],
        out_specs=vmem(),
        out_shape=jax.ShapeDtypeStruct((blocks, GRAM_ROWS, OWN), F32),
        scratch_shapes=[
            pltpu.VMEM((stars, cadences), F32),
            pltpu.VMEM((stars, cadences), jnp.int32),
            pltpu.VMEM((stars, cadences), jnp.int32),
            pltpu.VMEM((480, cadences), BF16),
            pltpu.SemaphoreType.DMA((3, stars // STEP)),
        ],
        compiler_params=params(58),
        cost_estimate=cost(2 * stars * cadences * 600, 14 * MIB),
        name="gram",
    )(flux, valid, quality, basis)

    parts, later_basis, later_decay, neighbours = lax.optimization_barrier(
        (parts, basis, decay, neighbours)
    )
    listed = lax.dynamic_slice_in_dim(neighbours, place * OWN, OWN, 0).reshape(blocks, -1)
    owner = listed >> 7
    spot = (owner & 15) + 16 * (owner >> 5) + 64 * (((owner >> 4) & 1) ^ lax.axis_index("c"))
    low_bits = (listed & 127) + 128 * (spot & 1)
    code = (spot >> 1) * 8 + lax.broadcasted_iota(jnp.int32, listed.shape, 1) // NEIGH

    cross_spec = pl.BlockSpec((CROSS_STEP, cadences), lambda i: (i, 0))
    table_spec = pl.BlockSpec((16, cadences), lambda i: (0, 0))
    crossed, decayed = pl.pallas_call(
        cross_kernel,
        grid=(stars // CROSS_STEP,),
        in_specs=[cross_spec, cross_spec, table_spec, table_spec, table_spec],
        out_specs=[
            pl.BlockSpec((CROSS_CHUNKS, CROSS_ROWS, OWN), lambda i: (i, 0, 0)),
            pl.BlockSpec((NOISE_TERMS, OWN), lambda i: (0, 0)),
        ],
        out_shape=[
            jax.ShapeDtypeStruct((blocks, CROSS_ROWS, OWN), F32),
            jax.ShapeDtypeStruct((NOISE_TERMS, OWN), F32),
        ],
        scratch_shapes=[pltpu.VMEM((560, cadences), BF16)],
        compiler_params=params(58),
        cost_estimate=cost(2 * stars * cadences * 800, 16 * MIB),
        name="cross",
    )(flux, valid, later_basis, later_decay, feed_w)
    parts = lax.all_to_all(parts, "tm", 0, 0, tiled=True)
    near_counts, far_counts = pl.pallas_call(
        count_kernel,
        in_specs=[vmem(), vmem()],
        out_specs=[vmem()] * 2,
        out_shape=[jax.ShapeDtypeStruct((32, OWN, 256), BF16)] * 2,
        compiler_params=params(16),
        cost_estimate=cost(4 << 30, 4 * MIB),
        name="count",
    )(code, low_bits)
    parts, crossed, decayed, near_counts, far_counts = lax.optimization_barrier(
        (parts, crossed, decayed, near_counts, far_counts)
    )

    nearby = ("y", "tm")
    copies = jax.ShapeDtypeStruct((lax.axis_size(nearby), 16, OWN), F32)
    fitted, kept = pl.pallas_call(
        solve_kernel,
        in_specs=[vmem()] * 2,
        out_specs=[vmem()] * 2,
        out_shape=[copies, jax.ShapeDtypeStruct((34, 16, OWN), F32)],
        scratch_shapes=[pltpu.VMEM((GRAM_ROWS, OWN), F32), pltpu.VMEM((256, OWN), F32)],
        compiler_params=params(16),
        cost_estimate=cost(1 << 20, 2 * MIB),
        name="solve",
    )(parts, prec)

    near = lax.all_to_all(fitted, nearby, 0, 0, tiled=True)
    near, last_decay, last_basis = lax.optimization_barrier((near, decay, basis))
    far = lax.ppermute(near, "c", [(0, 1), (1, 0)])
    begun = pl.pallas_call(
        near_kernel,
        in_specs=[vmem()] * 2,
        out_specs=vmem(),
        out_shape=jax.ShapeDtypeStruct((48, OWN), F32),
        compiler_params=params(16),
        cost_estimate=cost(1 << 28, 3 * MIB),
        name="near",
    )(near, near_counts)

    high, low, entry, stack = pl.pallas_call(
        noise_kernel,
        in_specs=[vmem()] * 4,
        out_specs=[vmem()] * 4,
        out_shape=[
            jax.ShapeDtypeStruct((cadences, cadences), BF16),
            jax.ShapeDtypeStruct((cadences, cadences), BF16),
            jax.ShapeDtypeStruct((96, cadences), BF16),
            jax.ShapeDtypeStruct((96, cadences), BF16),
        ],
        compiler_params=params(16),
        cost_estimate=cost(2 << 30, 2 * MIB),
        name="noise",
    )(last_decay, load_u, feed_w, last_basis)
    far, begun, high, low, entry, stack = lax.optimization_barrier(
        (far, begun, high, low, entry, stack)
    )
    rows = pl.pallas_call(
        map_kernel,
        in_specs=[vmem()] * 5,
        out_specs=vmem(),
        out_shape=jax.ShapeDtypeStruct((blocks, 16, OWN), F32),
        compiler_params=params(16),
        cost_estimate=cost(1 << 28, 6 * MIB),
        name="map",
    )(begun, far, far_counts, prec, kept)
    rows = lax.all_to_all(rows, "tm", 0, 0, tiled=True)

    carries = pl.pallas_call(
        carry_kernel,
        in_specs=[vmem()] * 3,
        out_specs=vmem(),
        out_shape=jax.ShapeDtypeStruct((blocks, 32, OWN), F32),
        compiler_params=params(16),
        cost_estimate=cost(1 << 24, 3 * MIB),
        name="local_carry",
    )(rows, crossed, decayed)
    carries = lax.all_to_all(carries, "tm", 0, 0, tiled=True)
    states = pl.pallas_call(
        state_kernel,
        in_specs=[vmem()],
        out_specs=vmem(),
        out_shape=jax.ShapeDtypeStruct((blocks, 16, OWN), F32),
        compiler_params=params(16),
        cost_estimate=cost(1 << 20, MIB),
        name="state",
    )(carries)
    states = lax.all_to_all(states, "tm", 0, 0, tiled=True)

    part_spec = pl.BlockSpec((WHITEN_CHUNKS, 16, OWN), lambda i: (i, 0, 0))
    coeffs, whitened = pl.pallas_call(
        whiten_kernel,
        grid=(stars // WHITEN_STEP,),
        in_specs=[vmem(), vmem(), part_spec, part_spec] + [vmem()] * 5,
        out_specs=[
            pl.BlockSpec((16, WHITEN_STEP), lambda i: (0, i)),
            pl.BlockSpec((WHITEN_STEP, cadences), lambda i: (i, 0)),
        ],
        out_shape=[
            jax.ShapeDtypeStruct((16, stars), F32),
            jax.ShapeDtypeStruct((stars, cadences), F32),
        ],
        compiler_params=params(32),
        cost_estimate=cost(2 * stars * cadences * 1700, 14 * MIB),
        name="whiten",
    )(flux, valid, rows, states, stack, entry, high, low, inv_diag[None, :])
    return coeffs.T, whitened


def solution(mesh):
    devices = mesh.devices
    split = Mesh(devices.reshape(devices.shape[0] // 2, 2, devices.shape[1]), ("y", "c", "tm"))
    star = ("y", "c")
    in_specs = (
        P(star, "tm"),
        P(star, "tm"),
        P(star, "tm"),
        P(None, "tm"),
        P(star, None),
        P(),
        P(None, "tm"),
        P(None, "tm"),
        P(None, "tm"),
        P("tm"),
    )
    out_specs = (P(star, None), P(star, "tm"))
    return jax.shard_map(
        per_device, mesh=split, in_specs=in_specs, out_specs=out_specs, check_vma=False
    )
```

```python
import jax
import jax.numpy as jnp
import numpy as np
from jax import lax
from jax.experimental import pallas as pl
from jax.experimental.pallas import tpu as pltpu
from jax.sharding import Mesh, PartitionSpec as P

BASIS_VECTORS = 16
NOISE_TERMS = 16
NEIGH = 64
DIAGONALS = 9
PAIRS = 136
OWN = 128
CUT = 128
STEP = 512
AHEAD = 2
CROSS_STEP = 512
CROSS_CHUNKS = CROSS_STEP // OWN
CHUNKS = STEP // OWN
GRAM_ROWS = PAIRS + 16
CROSS_ROWS = 16 + BASIS_VECTORS * NOISE_TERMS
WHITEN_STEP = 1024
WHITEN_CHUNKS = WHITEN_STEP // OWN

F32 = jnp.float32
BF16 = jnp.bfloat16
MIB = 1 << 20


def split3(x):
    high = x.astype(BF16)
    rest = x - high.astype(F32)
    mid = rest.astype(BF16)
    low = (rest - mid.astype(F32)).astype(BF16)
    return high, mid, low


def left_stack(x):
    high, mid, low = split3(x)
    return jnp.concatenate([high, high, mid, high, mid, low], axis=0)


def right_stack(x):
    high, mid, low = split3(x)
    return jnp.concatenate([high, mid, high, low, mid, high], axis=0)


def dot_nt(a, b):
    return lax.dot_general(a, b, (((1,), (1,)), ((), ())), preferred_element_type=F32)


def dot_tn(a, b):
    return lax.dot_general(a, b, (((0,), (0,)), ((), ())), preferred_element_type=F32)


def dot_nn(a, b):
    return lax.dot_general(a, b, (((1,), (0,)), ((), ())), preferred_element_type=F32)


def masked_sums(x, mask):
    rows = x.shape[0]
    stacked = jnp.concatenate(split3(x), axis=0)
    sums = dot_nn(stacked, mask.astype(F32).astype(BF16))
    return sums[0:rows] + (sums[rows : 2 * rows] + sums[2 * rows : 3 * rows])


def narrow_dots(table_ref, start, x, pieces):
    parts = split3(x)[:pieces]
    sums = [
        dot_nt(table_ref[start : start + 16 * (3 - place), :], part)
        for place, part in enumerate(parts)
    ]
    total = sums[0][32:48]
    for place in range(1, pieces):
        total = total + sums[place][16 * (2 - place) : 16 * (3 - place)]
    mid = sums[0][16:32] + sums[1][0:16]
    return sums[0][0:16] + (mid + total)


def gram_kernel(
    flux_hbm, valid_hbm, quality_hbm, basis_ref, out_ref, flux_ref, valid_ref, quality_ref, table_ref, arrived
):
    wide = DIAGONALS * BASIS_VECTORS
    rights = 3 * wide
    steps = flux_ref.shape[0] // STEP
    pairs = ((flux_hbm, flux_ref), (valid_hbm, valid_ref), (quality_hbm, quality_ref))

    def arrival(which, step):
        source, target = pairs[which]
        stars = pl.ds(step * STEP, STEP)
        return pltpu.make_async_copy(source.at[stars], target.at[stars], arrived.at[which, step])

    for step in range(AHEAD):
        for which in range(3):
            arrival(which, step).start()

    basis = basis_ref[...]
    scaled = basis * (1.0 / 12.0)
    products = []
    for diagonal in range(DIAGONALS):
        turned = basis
        if diagonal:
            turned = jnp.concatenate([basis[diagonal:], basis[:diagonal]], axis=0)
        products.append(scaled * turned)
    for place, piece in enumerate(split3(jnp.concatenate(products, axis=0))):
        table_ref[place * wide : (place + 1) * wide, :] = piece
    for place, piece in enumerate(split3(scaled)):
        table_ref[rights + place * 16 : rights + place * 16 + 16, :] = piece

    for step in range(steps):
        for which in range(3):
            arrival(which, step).wait()
            if step + AHEAD < steps:
                arrival(which, step + AHEAD).start()
        stars = slice(step * STEP, (step + 1) * STEP)
        quality = quality_ref[stars, :]
        twelfths = jnp.where(
            quality == 0, 12.0, jnp.where(quality == 1, 6.0, jnp.where(quality == 2, 4.0, 3.0))
        )
        weight = jnp.where(valid_ref[stars, :] != 0, twelfths, 0.0)
        grams = dot_nt(table_ref[0:rights, :], weight.astype(BF16))
        gram = grams[0:PAIRS] + (grams[wide : wide + PAIRS] + grams[2 * wide : 2 * wide + PAIRS])
        right = narrow_dots(table_ref, rights, weight * flux_ref[stars, :], 3)
        for chunk in range(CHUNKS):
            lanes = slice(chunk * OWN, (chunk + 1) * OWN)
            out_ref[step * CHUNKS + chunk, 0:PAIRS, :] = gram[:, lanes]
            out_ref[step * CHUNKS + chunk, PAIRS:GRAM_ROWS, :] = right[:, lanes]


def cross_kernel(
    flux_ref, valid_ref, basis_ref, decay_ref, feed_ref, out_ref, decayed_ref, table_ref
):
    cross = BASIS_VECTORS * NOISE_TERMS
    feeds = 2 * cross

    @pl.when(pl.program_id(0) == 0)
    def _():
        log_decay = jnp.log(decay_ref[...])
        count = log_decay.shape[1]
        rows = lax.broadcasted_iota(jnp.int32, (count, count), 0)
        columns = lax.broadcasted_iota(jnp.int32, (count, count), 1)
        suffix = masked_sums(log_decay, rows > columns)
        feed = jnp.exp(suffix) * feed_ref[...]
        whole = jnp.exp(suffix[:, 0:1] + log_decay[:, 0:1])
        decayed_ref[...] = jnp.broadcast_to(whole, (NOISE_TERMS, OWN))
        for k in range(BASIS_VECTORS):
            product = basis_ref[k : k + 1, :] * feed
            for place, piece in enumerate(split3(product)[:2]):
                first = place * cross + k * 16
                table_ref[first : first + 16, :] = piece
        for place, piece in enumerate(split3(feed)):
            table_ref[feeds + place * 16 : feeds + place * 16 + 16, :] = piece

    usable = valid_ref[...] != 0
    flux = flux_ref[...]
    sums = dot_nt(table_ref[0:feeds, :], jnp.where(usable, 1.0, 0.0).astype(BF16))
    crossed = sums[0:cross] + sums[cross : 2 * cross]
    plain = narrow_dots(table_ref, feeds, jnp.where(usable, flux, 0.0), 2)
    for chunk in range(CROSS_CHUNKS):
        lanes = slice(chunk * OWN, (chunk + 1) * OWN)
        out_ref[chunk, 0:16, :] = plain[:, lanes]
        out_ref[chunk, 16:CROSS_ROWS, :] = crossed[:, lanes]


def count_kernel(code_ref, low_ref, near_ref, far_ref):
    entries = 8 * NEIGH
    half, lows_all = near_ref.shape[0], near_ref.shape[2]
    row_code = lax.broadcasted_iota(jnp.int32, (2 * half * 8, entries), 0)
    low_code = lax.broadcasted_iota(jnp.int32, (lows_all, entries), 0)

    def one_half(group):
        code = code_ref[pl.ds(group, 1), :]
        low = low_ref[pl.ds(group, 1), :]
        highs = jnp.where(row_code == code, 1.0, 0.0).astype(BF16)
        lows = jnp.where(low_code == low, 1.0, 0.0).astype(BF16)
        return dot_nt(highs, lows).reshape(2 * half, 8, lows_all)

    def one(step, ignored):
        both = jnp.concatenate([one_half(2 * step), one_half(2 * step + 1)], axis=1).astype(BF16)
        span = pl.ds(pl.multiple_of(step * 16, 16), 16)
        near_ref[:, span, :] = both[:half]
        far_ref[:, span, :] = both[half:]
        return ignored

    lax.fori_loop(0, OWN // 16, one, 0)


def noise_kernel(
    decay_ref, load_ref, feed_ref, basis_ref, high_ref, low_ref, entry_ref, stack_ref
):
    log_decay = jnp.log(decay_ref[...])
    load = load_ref[...]
    feed = feed_ref[...]
    count = log_decay.shape[1]
    rows = lax.broadcasted_iota(jnp.int32, (count, count), 0)
    columns = lax.broadcasted_iota(jnp.int32, (count, count), 1)
    together = (rows // CUT) == (columns // CUT)
    before = masked_sums(log_decay, together & (rows < columns))
    tail = masked_sums(log_decay, together & (rows > columns))
    through = before + log_decay
    cuts = count // CUT
    totals = [through[:, (cut + 1) * CUT - 1 : (cut + 1) * CUT] for cut in range(cuts)]
    lower = lax.broadcasted_iota(jnp.int32, (CUT, CUT), 0) < lax.broadcasted_iota(
        jnp.int32, (CUT, CUT), 1
    )
    high_ref[...] = jnp.zeros_like(high_ref)
    low_ref[...] = jnp.zeros_like(low_ref)

    def keep(u, t, block):
        high = block.astype(BF16)
        span = (slice(u * CUT, (u + 1) * CUT), slice(t * CUT, (t + 1) * CUT))
        high_ref[span] = high
        low_ref[span] = (block - high.astype(F32)).astype(BF16)

    passed = jnp.zeros((NOISE_TERMS, 1), F32)
    entries = []
    for t in range(cuts):
        lanes = slice(t * CUT, (t + 1) * CUT)
        middle = through[:, t * CUT + CUT // 2 - 1 : t * CUT + CUT // 2]
        near_left = feed[:, lanes] * jnp.exp(middle - through[:, lanes])
        near_right = load[:, lanes] * jnp.exp(before[:, lanes] - middle)
        near = dot_tn(left_stack(near_left), right_stack(near_right))
        keep(t, t, jnp.where(lower, near, 0.0))
        far_right = right_stack(load[:, lanes] * jnp.exp(before[:, lanes]))
        between = jnp.zeros((NOISE_TERMS, 1), F32)
        for u in range(t - 1, -1, -1):
            span = slice(u * CUT, (u + 1) * CUT)
            far_left = left_stack(feed[:, span] * jnp.exp(tail[:, span] + between))
            keep(u, t, dot_tn(far_left, far_right))
            between = between + totals[u]
        entries.append(load[:, lanes] * jnp.exp(before[:, lanes] + passed))
        passed = passed + totals[t]
    entry_ref[...] = right_stack(jnp.concatenate(entries, axis=1))
    stack_ref[...] = right_stack(basis_ref[...])


def row_of_pair(i, j):
    apart = (j - i) % BASIS_VECTORS
    if apart < 8 or (apart == 8 and i < 8):
        return apart * BASIS_VECTORS + i
    return ((i - j) % BASIS_VECTORS) * BASIS_VECTORS + j


def eliminate(columns, vector):
    order = BASIS_VECTORS
    columns = list(columns)
    rows = lax.broadcasted_iota(jnp.int32, columns[0].shape, 0)
    scaled, pivots = [], []
    for k in range(order):
        inverse = 1.0 / columns[k][k : k + 1, :]
        factor = jnp.where(rows > k, columns[k] * inverse, 0.0)
        for j in range(k + 1, order):
            columns[j] = columns[j] - factor * columns[j][k : k + 1, :]
        scaled.append(factor)
        pivots.append(inverse)
        if vector is not None:
            vector = vector - factor * vector[k : k + 1, :]
    return scaled, pivots, vector, columns


def back_substitute(vector, uppers, pivots):
    rows = lax.broadcasted_iota(jnp.int32, vector.shape, 0)
    solved = jnp.zeros_like(vector)
    for k in range(BASIS_VECTORS - 1, -1, -1):
        value = vector[k : k + 1, :] * pivots[k]
        vector = vector - uppers[k] * value
        solved = jnp.where(rows == k, value, solved)
    return solved


def solve_kernel(parts_ref, prec_ref, fitted_ref, kept_ref, sums_ref, matrix_ref):
    total = parts_ref[0]
    for part in range(1, parts_ref.shape[0]):
        total = total + parts_ref[part]
    sums_ref[...] = total
    right = total[PAIRS : PAIRS + 16]
    kept_ref[33] = right
    order = BASIS_VECTORS
    for j in range(order):
        for i in range(order):
            row = row_of_pair(i, j)
            matrix_ref[j * order + i : j * order + i + 1, :] = sums_ref[row : row + 1, :]
    rows = lax.broadcasted_iota(jnp.int32, right.shape, 0)
    plain = [matrix_ref[j * order : (j + 1) * order, :] for j in range(order)]
    prec = prec_ref[...]
    ridged = [jnp.where(rows == j, plain[j] + 0.1, plain[j]) for j in range(order)]
    ignored, pivots, reduced, uppers = eliminate(ridged, right)
    fitted = back_substitute(reduced, uppers, pivots)
    for peer in range(fitted_ref.shape[0]):
        fitted_ref[peer] = fitted
    weighted = [jnp.where(rows == j, plain[j] + prec, plain[j]) for j in range(order)]
    factors, pivots, ignored, uppers = eliminate(weighted, None)
    for k in range(order):
        kept_ref[k] = factors[k]
        kept_ref[16 + k] = uppers[k]
        kept_ref[32, k : k + 1, :] = pivots[k]


def listed_sums(table_ref, counts_ref):
    sums = jnp.zeros((48, OWN), F32)
    for place in range(0, table_ref.shape[0], 2):
        wide = jnp.concatenate([table_ref[place], table_ref[place + 1]], axis=1)
        sums = sums + dot_nt(jnp.concatenate(split3(wide), axis=0), counts_ref[place // 2])
    return sums


def near_kernel(near_ref, counts_ref, out_ref):
    out_ref[...] = listed_sums(near_ref, counts_ref)


def map_kernel(begun_ref, far_ref, counts_ref, prec_ref, kept_ref, out_ref):
    prior = begun_ref[...] + listed_sums(far_ref, counts_ref)
    prior_mean = (prior[0:16] + (prior[16:32] + prior[32:48])) * (1.0 / NEIGH)
    vector = kept_ref[33] + prec_ref[...] * prior_mean
    for k in range(BASIS_VECTORS):
        vector = vector - kept_ref[k] * vector[k : k + 1, :]
    uppers = [kept_ref[16 + k] for k in range(BASIS_VECTORS)]
    pivots = [kept_ref[32, k : k + 1, :] for k in range(BASIS_VECTORS)]
    coeffs = back_substitute(vector, uppers, pivots)
    for peer in range(out_ref.shape[0]):
        out_ref[peer] = coeffs


def carry_kernel(rows_ref, crossed_ref, decayed_ref, out_ref):
    owners = rows_ref.shape[0]
    for owner in range(owners):
        coeffs = rows_ref[owner]
        carry = crossed_ref[owner, 0:16, :]
        for k in range(BASIS_VECTORS):
            first = 16 + 16 * k
            carry = carry - coeffs[k : k + 1, :] * crossed_ref[owner, first : first + 16, :]
        for peer in range(out_ref.shape[0]):
            out_ref[peer, owner] = carry
    for peer in range(out_ref.shape[0]):
        out_ref[peer, owners] = decayed_ref[...]


def entering(parts_ref, owner, place):
    last = parts_ref.shape[1] - 1
    state = jnp.zeros((NOISE_TERMS, OWN), F32)
    found = state
    for block in range(parts_ref.shape[0]):
        found = jnp.where(place == block, state, found)
        state = state * parts_ref[block, last] + parts_ref[block, owner]
    return found, state


def level_kernel(parts_ref, inner_ref, out_ref):
    place = lax.axis_index("z")
    owners = inner_ref.shape[0] - 1
    for owner in range(owners):
        found, state = entering(parts_ref, owner, place)
        inner_ref[owner] = found
        for peer in range(out_ref.shape[0]):
            out_ref[peer, owner] = state
    product = jnp.ones((NOISE_TERMS, OWN), F32)
    before = product
    for block in range(parts_ref.shape[0]):
        before = jnp.where(place == block, product, before)
        product = product * parts_ref[block, owners]
    inner_ref[owners] = before
    for peer in range(out_ref.shape[0]):
        out_ref[peer, owners] = product


def state_kernel(parts_ref, inner_ref, out_ref):
    place = lax.axis_index("x")
    owners = out_ref.shape[0]
    for owner in range(owners):
        found, ignored = entering(parts_ref, owner, place)
        out_ref[owner] = inner_ref[owner] + inner_ref[owners] * found


def whiten_kernel(
    flux_ref, valid_ref, rows_ref, states_ref, stack_ref, entry_ref, high_ref, low_ref, scale_ref, coeffs_ref, out_ref
):
    coeffs = jnp.concatenate([rows_ref[chunk] for chunk in range(WHITEN_CHUNKS)], axis=1)
    states = jnp.concatenate([states_ref[chunk] for chunk in range(WHITEN_CHUNKS)], axis=1)
    coeffs_ref[...] = coeffs
    trend = dot_tn(left_stack(coeffs), stack_ref[...])
    first = pl.multiple_of(pl.program_id(0) * WHITEN_STEP, WHITEN_STEP)
    stars = pl.ds(first, WHITEN_STEP)
    residual = jnp.where(valid_ref[stars, :] != 0, flux_ref[stars, :] - trend, 0.0)
    incoming = dot_tn(left_stack(states), entry_ref[...])
    high = residual.astype(BF16)
    low = (residual - high.astype(F32)).astype(BF16)
    count = residual.shape[1]
    for first in range(0, count, 256):
        lanes = slice(first, first + 256)
        upto = slice(0, first + 256)
        local = dot_nn(low[:, upto], high_ref[upto, lanes]) + dot_nn(high[:, upto], low_ref[upto, lanes])
        local = local + dot_nn(high[:, upto], high_ref[upto, lanes])
        out_ref[:, lanes] = (residual[:, lanes] - local - incoming[:, lanes]) * scale_ref[:, lanes]


def vmem():
    return pl.BlockSpec(memory_space=pltpu.VMEM)


def params(mib):
    return pltpu.CompilerParams(vmem_limit_bytes=mib * MIB)


def cost(flops, bytes_accessed):
    return pl.CostEstimate(flops=flops, bytes_accessed=bytes_accessed, transcendentals=0)


def per_device(
    flux, valid, quality, basis, neighbours, prior_prec, decay, load_u, feed_w, inv_diag
):
    stars, cadences = flux.shape
    blocks = stars // OWN
    cadence_axes = ("x", "z")
    place = lax.axis_index(cadence_axes)
    prec = jnp.broadcast_to(prior_prec[:, None], (BASIS_VECTORS, OWN))

    in_hbm = pl.BlockSpec(memory_space=pl.ANY)
    parts = pl.pallas_call(
        gram_kernel,
        in_specs=[in_hbm] * 3 + [vmem()],
        out_specs=vmem(),
        out_shape=jax.ShapeDtypeStruct((blocks, GRAM_ROWS, OWN), F32),
        scratch_shapes=[
            pltpu.VMEM((stars, cadences), F32),
            pltpu.VMEM((stars, cadences), jnp.int32),
            pltpu.VMEM((stars, cadences), jnp.int32),
            pltpu.VMEM((480, cadences), BF16),
            pltpu.SemaphoreType.DMA((3, stars // STEP)),
        ],
        compiler_params=params(58),
        cost_estimate=cost(2 * stars * cadences * 600, 14 * MIB),
        name="gram",
    )(flux, valid, quality, basis)

    parts, later_basis, later_decay, neighbours = lax.optimization_barrier(
        (parts, basis, decay, neighbours)
    )
    listed = lax.dynamic_slice_in_dim(neighbours, place * OWN, OWN, 0).reshape(blocks, -1)
    owner = listed >> 7
    spot = (owner & 15) + 16 * (owner >> 5) + 64 * (((owner >> 4) & 1) ^ lax.axis_index("c"))
    low_bits = (listed & 127) + 128 * (spot & 1)
    code = (spot >> 1) * 8 + lax.broadcasted_iota(jnp.int32, listed.shape, 1) // NEIGH

    cross_spec = pl.BlockSpec((CROSS_STEP, cadences), lambda i: (i, 0))
    table_spec = pl.BlockSpec((16, cadences), lambda i: (0, 0))
    crossed, decayed = pl.pallas_call(
        cross_kernel,
        grid=(stars // CROSS_STEP,),
        in_specs=[cross_spec, cross_spec, table_spec, table_spec, table_spec],
        out_specs=[
            pl.BlockSpec((CROSS_CHUNKS, CROSS_ROWS, OWN), lambda i: (i, 0, 0)),
            pl.BlockSpec((NOISE_TERMS, OWN), lambda i: (0, 0)),
        ],
        out_shape=[
            jax.ShapeDtypeStruct((blocks, CROSS_ROWS, OWN), F32),
            jax.ShapeDtypeStruct((NOISE_TERMS, OWN), F32),
        ],
        scratch_shapes=[pltpu.VMEM((560, cadences), BF16)],
        compiler_params=params(58),
        cost_estimate=cost(2 * stars * cadences * 800, 16 * MIB),
        name="cross",
    )(flux, valid, later_basis, later_decay, feed_w)
    parts = lax.all_to_all(parts, cadence_axes, 0, 0, tiled=True)
    near_counts, far_counts = pl.pallas_call(
        count_kernel,
        in_specs=[vmem(), vmem()],
        out_specs=[vmem()] * 2,
        out_shape=[jax.ShapeDtypeStruct((32, OWN, 256), BF16)] * 2,
        compiler_params=params(16),
        cost_estimate=cost(4 << 30, 4 * MIB),
        name="count",
    )(code, low_bits)
    parts, crossed, decayed, near_counts, far_counts = lax.optimization_barrier(
        (parts, crossed, decayed, near_counts, far_counts)
    )

    nearby = ("y", "x", "z")
    copies = jax.ShapeDtypeStruct((lax.axis_size(nearby), 16, OWN), F32)
    fitted, kept = pl.pallas_call(
        solve_kernel,
        in_specs=[vmem()] * 2,
        out_specs=[vmem()] * 2,
        out_shape=[copies, jax.ShapeDtypeStruct((34, 16, OWN), F32)],
        scratch_shapes=[pltpu.VMEM((GRAM_ROWS, OWN), F32), pltpu.VMEM((256, OWN), F32)],
        compiler_params=params(16),
        cost_estimate=cost(1 << 20, 2 * MIB),
        name="solve",
    )(parts, prec)

    near = lax.all_to_all(fitted, nearby, 0, 0, tiled=True)
    near, last_decay, last_basis = lax.optimization_barrier((near, decay, basis))
    far = lax.ppermute(near, "c", [(0, 1), (1, 0)])
    begun = pl.pallas_call(
        near_kernel,
        in_specs=[vmem()] * 2,
        out_specs=vmem(),
        out_shape=jax.ShapeDtypeStruct((48, OWN), F32),
        compiler_params=params(16),
        cost_estimate=cost(1 << 28, 3 * MIB),
        name="near",
    )(near, near_counts)

    high, low, entry, stack = pl.pallas_call(
        noise_kernel,
        in_specs=[vmem()] * 4,
        out_specs=[vmem()] * 4,
        out_shape=[
            jax.ShapeDtypeStruct((cadences, cadences), BF16),
            jax.ShapeDtypeStruct((cadences, cadences), BF16),
            jax.ShapeDtypeStruct((96, cadences), BF16),
            jax.ShapeDtypeStruct((96, cadences), BF16),
        ],
        compiler_params=params(16),
        cost_estimate=cost(2 << 30, 2 * MIB),
        name="noise",
    )(last_decay, load_u, feed_w, last_basis)
    far, begun, high, low, entry, stack = lax.optimization_barrier(
        (far, begun, high, low, entry, stack)
    )
    rows = pl.pallas_call(
        map_kernel,
        in_specs=[vmem()] * 5,
        out_specs=vmem(),
        out_shape=jax.ShapeDtypeStruct((blocks, 16, OWN), F32),
        compiler_params=params(16),
        cost_estimate=cost(1 << 28, 6 * MIB),
        name="map",
    )(begun, far, far_counts, prec, kept)
    rows = lax.all_to_all(rows, cadence_axes, 0, 0, tiled=True)

    along_z, along_x = lax.axis_size("z"), lax.axis_size("x")
    carries = pl.pallas_call(
        carry_kernel,
        in_specs=[vmem()] * 3,
        out_specs=vmem(),
        out_shape=jax.ShapeDtypeStruct((along_z, blocks + 1, 16, OWN), F32),
        compiler_params=params(16),
        cost_estimate=cost(1 << 24, 3 * MIB),
        name="local_carry",
    )(rows, crossed, decayed)
    carries = lax.all_to_all(carries, "z", 0, 0, tiled=True)
    inner, carries = pl.pallas_call(
        level_kernel,
        in_specs=[vmem()],
        out_specs=[vmem()] * 2,
        out_shape=[
            jax.ShapeDtypeStruct((blocks + 1, 16, OWN), F32),
            jax.ShapeDtypeStruct((along_x, blocks + 1, 16, OWN), F32),
        ],
        compiler_params=params(16),
        cost_estimate=cost(1 << 20, MIB),
        name="level",
    )(carries)
    carries = lax.all_to_all(carries, "x", 0, 0, tiled=True)
    states = pl.pallas_call(
        state_kernel,
        in_specs=[vmem()] * 2,
        out_specs=vmem(),
        out_shape=jax.ShapeDtypeStruct((blocks, 16, OWN), F32),
        compiler_params=params(16),
        cost_estimate=cost(1 << 20, MIB),
        name="state",
    )(carries, inner)

    part_spec = pl.BlockSpec((WHITEN_CHUNKS, 16, OWN), lambda i: (i, 0, 0))
    coeffs, whitened = pl.pallas_call(
        whiten_kernel,
        grid=(stars // WHITEN_STEP,),
        in_specs=[vmem(), vmem(), part_spec, part_spec] + [vmem()] * 5,
        out_specs=[
            pl.BlockSpec((16, WHITEN_STEP), lambda i: (0, i)),
            pl.BlockSpec((WHITEN_STEP, cadences), lambda i: (i, 0)),
        ],
        out_shape=[
            jax.ShapeDtypeStruct((16, stars), F32),
            jax.ShapeDtypeStruct((stars, cadences), F32),
        ],
        compiler_params=params(32),
        cost_estimate=cost(2 * stars * cadences * 1700, 14 * MIB),
        name="whiten",
    )(flux, valid, rows, states, stack, entry, high, low, inv_diag[None, :])
    return coeffs.T, whitened


def solution(mesh):
    devices = mesh.devices
    split = Mesh(devices.reshape(devices.shape[0] // 2, 2, 4, devices.shape[1] // 4), ("y", "c", "x", "z"))
    tm = ("x", "z")
    star = ("y", "c")
    in_specs = (
        P(star, tm),
        P(star, tm),
        P(star, tm),
        P(None, tm),
        P(star, None),
        P(),
        P(None, tm),
        P(None, tm),
        P(None, tm),
        P(tm),
    )
    out_specs = (P(star, None), P(star, tm))
    return jax.shard_map(
        per_device, mesh=split, in_specs=in_specs, out_specs=out_specs, check_vma=False
    )
```

```python
import jax
import jax.numpy as jnp
import numpy as np
from jax import lax
from jax.experimental import pallas as pl
from jax.experimental.pallas import tpu as pltpu
from jax.sharding import Mesh, PartitionSpec as P

BASIS_VECTORS = 16
NOISE_TERMS = 16
NEIGH = 64
DIAGONALS = 9
PAIRS = 136
OWN = 128
CUT = 128
STEP = 512
AHEAD = 2
CROSS_STEP = 512
CROSS_CHUNKS = CROSS_STEP // OWN
CHUNKS = STEP // OWN
GRAM_ROWS = PAIRS + 16
CROSS_ROWS = 16 + BASIS_VECTORS * NOISE_TERMS
WHITEN_STEP = 1024
WHITEN_CHUNKS = WHITEN_STEP // OWN

F32 = jnp.float32
BF16 = jnp.bfloat16
MIB = 1 << 20


def split3(x):
    high = x.astype(BF16)
    rest = x - high.astype(F32)
    mid = rest.astype(BF16)
    low = (rest - mid.astype(F32)).astype(BF16)
    return high, mid, low


def left_stack(x):
    high, mid, low = split3(x)
    return jnp.concatenate([high, high, mid, high, mid, low], axis=0)


def right_stack(x):
    high, mid, low = split3(x)
    return jnp.concatenate([high, mid, high, low, mid, high], axis=0)


def dot_nt(a, b):
    return lax.dot_general(a, b, (((1,), (1,)), ((), ())), preferred_element_type=F32)


def dot_tn(a, b):
    return lax.dot_general(a, b, (((0,), (0,)), ((), ())), preferred_element_type=F32)


def dot_nn(a, b):
    return lax.dot_general(a, b, (((1,), (0,)), ((), ())), preferred_element_type=F32)


def masked_sums(x, mask):
    rows = x.shape[0]
    stacked = jnp.concatenate(split3(x), axis=0)
    sums = dot_nn(stacked, mask.astype(F32).astype(BF16))
    return sums[0:rows] + (sums[rows : 2 * rows] + sums[2 * rows : 3 * rows])


def narrow_dots(table_ref, start, x, pieces):
    parts = split3(x)[:pieces]
    sums = [
        dot_nt(table_ref[start : start + 16 * (3 - place), :], part)
        for place, part in enumerate(parts)
    ]
    total = sums[0][32:48]
    for place in range(1, pieces):
        total = total + sums[place][16 * (2 - place) : 16 * (3 - place)]
    mid = sums[0][16:32] + sums[1][0:16]
    return sums[0][0:16] + (mid + total)


def gram_kernel(
    flux_hbm, valid_hbm, quality_hbm, basis_ref, out_ref, flux_ref, valid_ref, quality_ref, table_ref, arrived
):
    wide = DIAGONALS * BASIS_VECTORS
    rights = 3 * wide
    steps = flux_ref.shape[0] // STEP
    pairs = ((flux_hbm, flux_ref), (valid_hbm, valid_ref), (quality_hbm, quality_ref))

    def arrival(which, step):
        source, target = pairs[which]
        stars = pl.ds(step * STEP, STEP)
        return pltpu.make_async_copy(source.at[stars], target.at[stars], arrived.at[which, step])

    for step in range(AHEAD):
        for which in range(3):
            arrival(which, step).start()

    basis = basis_ref[...]
    scaled = basis * (1.0 / 12.0)
    products = []
    for diagonal in range(DIAGONALS):
        turned = basis
        if diagonal:
            turned = jnp.concatenate([basis[diagonal:], basis[:diagonal]], axis=0)
        products.append(scaled * turned)
    for place, piece in enumerate(split3(jnp.concatenate(products, axis=0))):
        table_ref[place * wide : (place + 1) * wide, :] = piece
    for place, piece in enumerate(split3(scaled)):
        table_ref[rights + place * 16 : rights + place * 16 + 16, :] = piece

    for step in range(steps):
        for which in range(3):
            arrival(which, step).wait()
            if step + AHEAD < steps:
                arrival(which, step + AHEAD).start()
        stars = slice(step * STEP, (step + 1) * STEP)
        quality = quality_ref[stars, :]
        twelfths = jnp.where(
            quality == 0, 12.0, jnp.where(quality == 1, 6.0, jnp.where(quality == 2, 4.0, 3.0))
        )
        weight = jnp.where(valid_ref[stars, :] != 0, twelfths, 0.0)
        grams = dot_nt(table_ref[0:rights, :], weight.astype(BF16))
        gram = grams[0:PAIRS] + (grams[wide : wide + PAIRS] + grams[2 * wide : 2 * wide + PAIRS])
        right = narrow_dots(table_ref, rights, weight * flux_ref[stars, :], 3)
        for chunk in range(CHUNKS):
            lanes = slice(chunk * OWN, (chunk + 1) * OWN)
            out_ref[step * CHUNKS + chunk, 0:PAIRS, :] = gram[:, lanes]
            out_ref[step * CHUNKS + chunk, PAIRS:GRAM_ROWS, :] = right[:, lanes]


def cross_kernel(
    flux_ref, valid_ref, basis_ref, decay_ref, feed_ref, out_ref, decayed_ref, table_ref
):
    cross = BASIS_VECTORS * NOISE_TERMS
    feeds = 2 * cross

    @pl.when(pl.program_id(0) == 0)
    def _():
        log_decay = jnp.log(decay_ref[...])
        count = log_decay.shape[1]
        rows = lax.broadcasted_iota(jnp.int32, (count, count), 0)
        columns = lax.broadcasted_iota(jnp.int32, (count, count), 1)
        suffix = masked_sums(log_decay, rows > columns)
        feed = jnp.exp(suffix) * feed_ref[...]
        whole = jnp.exp(suffix[:, 0:1] + log_decay[:, 0:1])
        decayed_ref[...] = jnp.broadcast_to(whole, (NOISE_TERMS, OWN))
        for k in range(BASIS_VECTORS):
            product = basis_ref[k : k + 1, :] * feed
            for place, piece in enumerate(split3(product)[:2]):
                first = place * cross + k * 16
                table_ref[first : first + 16, :] = piece
        for place, piece in enumerate(split3(feed)):
            table_ref[feeds + place * 16 : feeds + place * 16 + 16, :] = piece

    usable = valid_ref[...] != 0
    flux = flux_ref[...]
    sums = dot_nt(table_ref[0:feeds, :], jnp.where(usable, 1.0, 0.0).astype(BF16))
    crossed = sums[0:cross] + sums[cross : 2 * cross]
    plain = narrow_dots(table_ref, feeds, jnp.where(usable, flux, 0.0), 2)
    for chunk in range(CROSS_CHUNKS):
        lanes = slice(chunk * OWN, (chunk + 1) * OWN)
        out_ref[chunk, 0:16, :] = plain[:, lanes]
        out_ref[chunk, 16:CROSS_ROWS, :] = crossed[:, lanes]


def count_kernel(code_ref, low_ref, near_ref, far_ref):
    entries = 8 * NEIGH
    half, lows_all = near_ref.shape[0], near_ref.shape[2]
    row_code = lax.broadcasted_iota(jnp.int32, (2 * half * 8, entries), 0)
    low_code = lax.broadcasted_iota(jnp.int32, (lows_all, entries), 0)

    def one_half(group):
        code = code_ref[pl.ds(group, 1), :]
        low = low_ref[pl.ds(group, 1), :]
        highs = jnp.where(row_code == code, 1.0, 0.0).astype(BF16)
        lows = jnp.where(low_code == low, 1.0, 0.0).astype(BF16)
        return dot_nt(highs, lows).reshape(2 * half, 8, lows_all)

    def one(step, ignored):
        both = jnp.concatenate([one_half(2 * step), one_half(2 * step + 1)], axis=1).astype(BF16)
        span = pl.ds(pl.multiple_of(step * 16, 16), 16)
        near_ref[:, span, :] = both[:half]
        far_ref[:, span, :] = both[half:]
        return ignored

    lax.fori_loop(0, OWN // 16, one, 0)


def noise_kernel(
    decay_ref, load_ref, feed_ref, basis_ref, high_ref, low_ref, entry_ref, stack_ref
):
    log_decay = jnp.log(decay_ref[...])
    load = load_ref[...]
    feed = feed_ref[...]
    count = log_decay.shape[1]
    rows = lax.broadcasted_iota(jnp.int32, (count, count), 0)
    columns = lax.broadcasted_iota(jnp.int32, (count, count), 1)
    together = (rows // CUT) == (columns // CUT)
    before = masked_sums(log_decay, together & (rows < columns))
    tail = masked_sums(log_decay, together & (rows > columns))
    through = before + log_decay
    cuts = count // CUT
    totals = [through[:, (cut + 1) * CUT - 1 : (cut + 1) * CUT] for cut in range(cuts)]
    lower = lax.broadcasted_iota(jnp.int32, (CUT, CUT), 0) < lax.broadcasted_iota(
        jnp.int32, (CUT, CUT), 1
    )
    high_ref[...] = jnp.zeros_like(high_ref)
    low_ref[...] = jnp.zeros_like(low_ref)

    def keep(u, t, block):
        high = block.astype(BF16)
        span = (slice(u * CUT, (u + 1) * CUT), slice(t * CUT, (t + 1) * CUT))
        high_ref[span] = high
        low_ref[span] = (block - high.astype(F32)).astype(BF16)

    passed = jnp.zeros((NOISE_TERMS, 1), F32)
    entries = []
    for t in range(cuts):
        lanes = slice(t * CUT, (t + 1) * CUT)
        middle = through[:, t * CUT + CUT // 2 - 1 : t * CUT + CUT // 2]
        near_left = feed[:, lanes] * jnp.exp(middle - through[:, lanes])
        near_right = load[:, lanes] * jnp.exp(before[:, lanes] - middle)
        near = dot_tn(left_stack(near_left), right_stack(near_right))
        keep(t, t, jnp.where(lower, near, 0.0))
        far_right = right_stack(load[:, lanes] * jnp.exp(before[:, lanes]))
        between = jnp.zeros((NOISE_TERMS, 1), F32)
        for u in range(t - 1, -1, -1):
            span = slice(u * CUT, (u + 1) * CUT)
            far_left = left_stack(feed[:, span] * jnp.exp(tail[:, span] + between))
            keep(u, t, dot_tn(far_left, far_right))
            between = between + totals[u]
        entries.append(load[:, lanes] * jnp.exp(before[:, lanes] + passed))
        passed = passed + totals[t]
    entry_ref[...] = right_stack(jnp.concatenate(entries, axis=1))
    stack_ref[...] = right_stack(basis_ref[...])


def row_of_pair(i, j):
    apart = (j - i) % BASIS_VECTORS
    if apart < 8 or (apart == 8 and i < 8):
        return apart * BASIS_VECTORS + i
    return ((i - j) % BASIS_VECTORS) * BASIS_VECTORS + j


def eliminate(columns, vector):
    order = BASIS_VECTORS
    columns = list(columns)
    rows = lax.broadcasted_iota(jnp.int32, columns[0].shape, 0)
    scaled, pivots = [], []
    for k in range(order):
        inverse = 1.0 / columns[k][k : k + 1, :]
        factor = jnp.where(rows > k, columns[k] * inverse, 0.0)
        for j in range(k + 1, order):
            columns[j] = columns[j] - factor * columns[j][k : k + 1, :]
        scaled.append(factor)
        pivots.append(inverse)
        if vector is not None:
            vector = vector - factor * vector[k : k + 1, :]
    return scaled, pivots, vector, columns


def back_substitute(vector, uppers, pivots):
    rows = lax.broadcasted_iota(jnp.int32, vector.shape, 0)
    solved = jnp.zeros_like(vector)
    for k in range(BASIS_VECTORS - 1, -1, -1):
        value = vector[k : k + 1, :] * pivots[k]
        vector = vector - uppers[k] * value
        solved = jnp.where(rows == k, value, solved)
    return solved


def solve_kernel(parts_ref, prec_ref, fitted_ref, kept_ref, sums_ref, matrix_ref):
    total = parts_ref[0]
    for part in range(1, parts_ref.shape[0]):
        total = total + parts_ref[part]
    sums_ref[...] = total
    right = total[PAIRS : PAIRS + 16]
    kept_ref[33] = right
    order = BASIS_VECTORS
    for j in range(order):
        for i in range(order):
            row = row_of_pair(i, j)
            matrix_ref[j * order + i : j * order + i + 1, :] = sums_ref[row : row + 1, :]
    rows = lax.broadcasted_iota(jnp.int32, right.shape, 0)
    plain = [matrix_ref[j * order : (j + 1) * order, :] for j in range(order)]
    prec = prec_ref[...]
    ridged = [jnp.where(rows == j, plain[j] + 0.1, plain[j]) for j in range(order)]
    ignored, pivots, reduced, uppers = eliminate(ridged, right)
    fitted = back_substitute(reduced, uppers, pivots)
    for peer in range(fitted_ref.shape[0]):
        fitted_ref[peer] = fitted
    weighted = [jnp.where(rows == j, plain[j] + prec, plain[j]) for j in range(order)]
    factors, pivots, ignored, uppers = eliminate(weighted, None)
    for k in range(order):
        kept_ref[k] = factors[k]
        kept_ref[16 + k] = uppers[k]
        kept_ref[32, k : k + 1, :] = pivots[k]


def listed_sums(table_ref, counts_ref):
    sums = jnp.zeros((48, OWN), F32)
    for place in range(0, table_ref.shape[0], 2):
        wide = jnp.concatenate([table_ref[place], table_ref[place + 1]], axis=1)
        sums = sums + dot_nt(jnp.concatenate(split3(wide), axis=0), counts_ref[place // 2])
    return sums


def near_kernel(near_ref, counts_ref, out_ref):
    out_ref[...] = listed_sums(near_ref, counts_ref)


def map_kernel(begun_ref, far_ref, counts_ref, prec_ref, kept_ref, out_ref):
    prior = begun_ref[...] + listed_sums(far_ref, counts_ref)
    prior_mean = (prior[0:16] + (prior[16:32] + prior[32:48])) * (1.0 / NEIGH)
    vector = kept_ref[33] + prec_ref[...] * prior_mean
    for k in range(BASIS_VECTORS):
        vector = vector - kept_ref[k] * vector[k : k + 1, :]
    uppers = [kept_ref[16 + k] for k in range(BASIS_VECTORS)]
    pivots = [kept_ref[32, k : k + 1, :] for k in range(BASIS_VECTORS)]
    coeffs = back_substitute(vector, uppers, pivots)
    for peer in range(out_ref.shape[0]):
        out_ref[peer] = coeffs


def carry_kernel(rows_ref, crossed_ref, decayed_ref, out_ref):
    owners = rows_ref.shape[0]
    for owner in range(owners):
        coeffs = rows_ref[owner]
        carry = crossed_ref[owner, 0:16, :]
        for k in range(BASIS_VECTORS):
            first = 16 + 16 * k
            carry = carry - coeffs[k : k + 1, :] * crossed_ref[owner, first : first + 16, :]
        out_ref[owner] = carry
    out_ref[owners] = decayed_ref[...]


def level_kernel(own_ref, first_ref, second_ref, third_ref, inner_ref, out_ref):
    place = lax.axis_index("z")
    refs = (own_ref, first_ref, second_ref, third_ref)
    around = len(refs)
    owners = own_ref.shape[0] - 1

    def of_block(block, row):
        value = refs[0][row]
        for back in range(1, around):
            value = jnp.where(lax.rem(place + around - back, around) == block, refs[back][row], value)
        return value

    decays = [of_block(block, owners) for block in range(around)]
    for owner in range(owners):
        state = jnp.zeros((NOISE_TERMS, OWN), F32)
        found = state
        for block in range(around):
            found = jnp.where(place == block, state, found)
            state = state * decays[block] + of_block(block, owner)
        inner_ref[owner] = found
        out_ref[owner] = state
    product = jnp.ones((NOISE_TERMS, OWN), F32)
    before = product
    for block in range(around):
        before = jnp.where(place == block, product, before)
        product = product * decays[block]
    inner_ref[owners] = before
    out_ref[owners] = product


def state_kernel(first_ref, second_ref, third_ref, inner_ref, out_ref):
    owners = out_ref.shape[0]
    for owner in range(owners):
        state = second_ref[owner] + second_ref[owners] * third_ref[owner]
        state = first_ref[owner] + first_ref[owners] * state
        out_ref[owner] = inner_ref[owner] + inner_ref[owners] * state


def whiten_kernel(
    flux_ref, valid_ref, rows_ref, states_ref, stack_ref, entry_ref, high_ref, low_ref, scale_ref, coeffs_ref, out_ref
):
    coeffs = jnp.concatenate([rows_ref[chunk] for chunk in range(WHITEN_CHUNKS)], axis=1)
    states = jnp.concatenate([states_ref[chunk] for chunk in range(WHITEN_CHUNKS)], axis=1)
    coeffs_ref[...] = coeffs
    trend = dot_tn(left_stack(coeffs), stack_ref[...])
    first = pl.multiple_of(pl.program_id(0) * WHITEN_STEP, WHITEN_STEP)
    stars = pl.ds(first, WHITEN_STEP)
    residual = jnp.where(valid_ref[stars, :] != 0, flux_ref[stars, :] - trend, 0.0)
    incoming = dot_tn(left_stack(states), entry_ref[...])
    high = residual.astype(BF16)
    low = (residual - high.astype(F32)).astype(BF16)
    count = residual.shape[1]
    for first in range(0, count, 256):
        lanes = slice(first, first + 256)
        upto = slice(0, first + 256)
        local = dot_nn(low[:, upto], high_ref[upto, lanes]) + dot_nn(high[:, upto], low_ref[upto, lanes])
        local = local + dot_nn(high[:, upto], high_ref[upto, lanes])
        out_ref[:, lanes] = (residual[:, lanes] - local - incoming[:, lanes]) * scale_ref[:, lanes]


def vmem():
    return pl.BlockSpec(memory_space=pltpu.VMEM)


def params(mib):
    return pltpu.CompilerParams(vmem_limit_bytes=mib * MIB)


def cost(flops, bytes_accessed):
    return pl.CostEstimate(flops=flops, bytes_accessed=bytes_accessed, transcendentals=0)


def per_device(
    flux, valid, quality, basis, neighbours, prior_prec, decay, load_u, feed_w, inv_diag
):
    stars, cadences = flux.shape
    blocks = stars // OWN
    cadence_axes = ("x", "z")
    place = lax.axis_index(cadence_axes)
    prec = jnp.broadcast_to(prior_prec[:, None], (BASIS_VECTORS, OWN))

    in_hbm = pl.BlockSpec(memory_space=pl.ANY)
    parts = pl.pallas_call(
        gram_kernel,
        in_specs=[in_hbm] * 3 + [vmem()],
        out_specs=vmem(),
        out_shape=jax.ShapeDtypeStruct((blocks, GRAM_ROWS, OWN), F32),
        scratch_shapes=[
            pltpu.VMEM((stars, cadences), F32),
            pltpu.VMEM((stars, cadences), jnp.int32),
            pltpu.VMEM((stars, cadences), jnp.int32),
            pltpu.VMEM((480, cadences), BF16),
            pltpu.SemaphoreType.DMA((3, stars // STEP)),
        ],
        compiler_params=params(58),
        cost_estimate=cost(2 * stars * cadences * 600, 14 * MIB),
        name="gram",
    )(flux, valid, quality, basis)

    parts, later_basis, later_decay, neighbours = lax.optimization_barrier(
        (parts, basis, decay, neighbours)
    )
    listed = lax.dynamic_slice_in_dim(neighbours, place * OWN, OWN, 0).reshape(blocks, -1)
    owner = listed >> 7
    spot = (owner & 15) + 16 * (owner >> 5) + 64 * (((owner >> 4) & 1) ^ lax.axis_index("c"))
    low_bits = (listed & 127) + 128 * (spot & 1)
    code = (spot >> 1) * 8 + lax.broadcasted_iota(jnp.int32, listed.shape, 1) // NEIGH

    cross_spec = pl.BlockSpec((CROSS_STEP, cadences), lambda i: (i, 0))
    table_spec = pl.BlockSpec((16, cadences), lambda i: (0, 0))
    crossed, decayed = pl.pallas_call(
        cross_kernel,
        grid=(stars // CROSS_STEP,),
        in_specs=[cross_spec, cross_spec, table_spec, table_spec, table_spec],
        out_specs=[
            pl.BlockSpec((CROSS_CHUNKS, CROSS_ROWS, OWN), lambda i: (i, 0, 0)),
            pl.BlockSpec((NOISE_TERMS, OWN), lambda i: (0, 0)),
        ],
        out_shape=[
            jax.ShapeDtypeStruct((blocks, CROSS_ROWS, OWN), F32),
            jax.ShapeDtypeStruct((NOISE_TERMS, OWN), F32),
        ],
        scratch_shapes=[pltpu.VMEM((560, cadences), BF16)],
        compiler_params=params(58),
        cost_estimate=cost(2 * stars * cadences * 800, 16 * MIB),
        name="cross",
    )(flux, valid, later_basis, later_decay, feed_w)
    parts = lax.all_to_all(parts, cadence_axes, 0, 0, tiled=True)
    near_counts, far_counts = pl.pallas_call(
        count_kernel,
        in_specs=[vmem(), vmem()],
        out_specs=[vmem()] * 2,
        out_shape=[jax.ShapeDtypeStruct((32, OWN, 256), BF16)] * 2,
        compiler_params=params(16),
        cost_estimate=cost(4 << 30, 4 * MIB),
        name="count",
    )(code, low_bits)
    parts, crossed, decayed, near_counts, far_counts = lax.optimization_barrier(
        (parts, crossed, decayed, near_counts, far_counts)
    )

    nearby = ("y", "x", "z")
    copies = jax.ShapeDtypeStruct((lax.axis_size(nearby), 16, OWN), F32)
    fitted, kept = pl.pallas_call(
        solve_kernel,
        in_specs=[vmem()] * 2,
        out_specs=[vmem()] * 2,
        out_shape=[copies, jax.ShapeDtypeStruct((34, 16, OWN), F32)],
        scratch_shapes=[pltpu.VMEM((GRAM_ROWS, OWN), F32), pltpu.VMEM((256, OWN), F32)],
        compiler_params=params(16),
        cost_estimate=cost(1 << 20, 2 * MIB),
        name="solve",
    )(parts, prec)

    near = lax.all_to_all(fitted, nearby, 0, 0, tiled=True)
    near, last_decay, last_basis = lax.optimization_barrier((near, decay, basis))
    far = lax.ppermute(near, "c", [(0, 1), (1, 0)])
    begun = pl.pallas_call(
        near_kernel,
        in_specs=[vmem()] * 2,
        out_specs=vmem(),
        out_shape=jax.ShapeDtypeStruct((48, OWN), F32),
        compiler_params=params(16),
        cost_estimate=cost(1 << 28, 3 * MIB),
        name="near",
    )(near, near_counts)

    high, low, entry, stack = pl.pallas_call(
        noise_kernel,
        in_specs=[vmem()] * 4,
        out_specs=[vmem()] * 4,
        out_shape=[
            jax.ShapeDtypeStruct((cadences, cadences), BF16),
            jax.ShapeDtypeStruct((cadences, cadences), BF16),
            jax.ShapeDtypeStruct((96, cadences), BF16),
            jax.ShapeDtypeStruct((96, cadences), BF16),
        ],
        compiler_params=params(16),
        cost_estimate=cost(2 << 30, 2 * MIB),
        name="noise",
    )(last_decay, load_u, feed_w, last_basis)
    far, begun, high, low, entry, stack = lax.optimization_barrier(
        (far, begun, high, low, entry, stack)
    )
    rows = pl.pallas_call(
        map_kernel,
        in_specs=[vmem()] * 5,
        out_specs=vmem(),
        out_shape=jax.ShapeDtypeStruct((blocks, 16, OWN), F32),
        compiler_params=params(16),
        cost_estimate=cost(1 << 28, 6 * MIB),
        name="map",
    )(begun, far, far_counts, prec, kept)
    rows = lax.all_to_all(rows, cadence_axes, 0, 0, tiled=True)

    block_shape = jax.ShapeDtypeStruct((blocks + 1, 16, OWN), F32)
    carries = pl.pallas_call(
        carry_kernel,
        in_specs=[vmem()] * 3,
        out_specs=vmem(),
        out_shape=block_shape,
        compiler_params=params(16),
        cost_estimate=cost(1 << 24, 3 * MIB),
        name="local_carry",
    )(rows, crossed, decayed)
    along_z, along_x = lax.axis_size("z"), lax.axis_size("x")
    rings = [
        lax.ppermute(carries, "z", [(i, (i + back) % along_z) for i in range(along_z)])
        for back in range(1, along_z)
    ]
    inner, lines = pl.pallas_call(
        level_kernel,
        in_specs=[vmem()] * 4,
        out_specs=[vmem()] * 2,
        out_shape=[block_shape] * 2,
        compiler_params=params(16),
        cost_estimate=cost(1 << 20, MIB),
        name="level",
    )(carries, *rings)
    earlier = [
        lax.ppermute(lines, "x", [(i, i + back) for i in range(along_x - back)])
        for back in range(1, along_x)
    ]
    states = pl.pallas_call(
        state_kernel,
        in_specs=[vmem()] * 4,
        out_specs=vmem(),
        out_shape=jax.ShapeDtypeStruct((blocks, 16, OWN), F32),
        compiler_params=params(16),
        cost_estimate=cost(1 << 20, MIB),
        name="state",
    )(*earlier, inner)

    part_spec = pl.BlockSpec((WHITEN_CHUNKS, 16, OWN), lambda i: (i, 0, 0))
    coeffs, whitened = pl.pallas_call(
        whiten_kernel,
        grid=(stars // WHITEN_STEP,),
        in_specs=[vmem(), vmem(), part_spec, part_spec] + [vmem()] * 5,
        out_specs=[
            pl.BlockSpec((16, WHITEN_STEP), lambda i: (0, i)),
            pl.BlockSpec((WHITEN_STEP, cadences), lambda i: (i, 0)),
        ],
        out_shape=[
            jax.ShapeDtypeStruct((16, stars), F32),
            jax.ShapeDtypeStruct((stars, cadences), F32),
        ],
        compiler_params=params(32),
        cost_estimate=cost(2 * stars * cadences * 1700, 14 * MIB),
        name="whiten",
    )(flux, valid, rows, states, stack, entry, high, low, inv_diag[None, :])
    return coeffs.T, whitened


def solution(mesh):
    devices = mesh.devices
    split = Mesh(devices.reshape(devices.shape[0] // 2, 2, 4, devices.shape[1] // 4), ("y", "c", "x", "z"))
    tm = ("x", "z")
    star = ("y", "c")
    in_specs = (
        P(star, tm),
        P(star, tm),
        P(star, tm),
        P(None, tm),
        P(star, None),
        P(),
        P(None, tm),
        P(None, tm),
        P(None, tm),
        P(tm),
    )
    out_specs = (P(star, None), P(star, tm))
    return jax.shard_map(
        per_device, mesh=split, in_specs=in_specs, out_specs=out_specs, check_vma=False
    )
```

```python
import jax
import jax.numpy as jnp
import numpy as np
from jax import lax
from jax.experimental import pallas as pl
from jax.experimental.pallas import tpu as pltpu
from jax.sharding import Mesh, PartitionSpec as P

BASIS_VECTORS = 16
NOISE_TERMS = 16
NEIGH = 64
DIAGONALS = 9
PAIRS = 136
OWN = 128
CUT = 128
STEP = 512
AHEAD = 2
CROSS_STEP = 512
CROSS_CHUNKS = CROSS_STEP // OWN
CHUNKS = STEP // OWN
GRAM_ROWS = PAIRS + 16
CROSS_ROWS = 16 + BASIS_VECTORS * NOISE_TERMS
WHITEN_STEP = 512
FINISH_STEP = 512
FINISH_CHUNKS = FINISH_STEP // OWN
WHITEN_CHUNKS = WHITEN_STEP // OWN

F32 = jnp.float32
BF16 = jnp.bfloat16
MIB = 1 << 20


def split3(x):
    high = x.astype(BF16)
    rest = x - high.astype(F32)
    mid = rest.astype(BF16)
    low = (rest - mid.astype(F32)).astype(BF16)
    return high, mid, low


def left_stack(x):
    high, mid, low = split3(x)
    return jnp.concatenate([high, high, mid, high, mid, low], axis=0)


def right_stack(x):
    high, mid, low = split3(x)
    return jnp.concatenate([high, mid, high, low, mid, high], axis=0)


def dot_nt(a, b):
    return lax.dot_general(a, b, (((1,), (1,)), ((), ())), preferred_element_type=F32)


def dot_tn(a, b):
    return lax.dot_general(a, b, (((0,), (0,)), ((), ())), preferred_element_type=F32)


def dot_nn(a, b):
    return lax.dot_general(a, b, (((1,), (0,)), ((), ())), preferred_element_type=F32)


def masked_sums(x, mask):
    rows = x.shape[0]
    stacked = jnp.concatenate(split3(x), axis=0)
    sums = dot_nn(stacked, mask.astype(F32).astype(BF16))
    return sums[0:rows] + (sums[rows : 2 * rows] + sums[2 * rows : 3 * rows])


def narrow_dots(table_ref, start, x, pieces):
    parts = split3(x)[:pieces]
    sums = [
        dot_nt(table_ref[start : start + 16 * (3 - place), :], part)
        for place, part in enumerate(parts)
    ]
    total = sums[0][32:48]
    for place in range(1, pieces):
        total = total + sums[place][16 * (2 - place) : 16 * (3 - place)]
    mid = sums[0][16:32] + sums[1][0:16]
    return sums[0][0:16] + (mid + total)


def gram_kernel(
    flux_hbm, valid_hbm, quality_hbm, basis_ref, out_ref, flux_ref, valid_ref, quality_ref, table_ref, arrived
):
    wide = DIAGONALS * BASIS_VECTORS
    rights = 3 * wide
    steps = flux_ref.shape[0] // STEP
    pairs = ((flux_hbm, flux_ref), (valid_hbm, valid_ref), (quality_hbm, quality_ref))

    def arrival(which, step):
        source, target = pairs[which]
        stars = pl.ds(step * STEP, STEP)
        return pltpu.make_async_copy(source.at[stars], target.at[stars], arrived.at[which, step])

    for step in range(AHEAD):
        for which in range(3):
            arrival(which, step).start()

    basis = basis_ref[...]
    scaled = basis * (1.0 / 12.0)
    products = []
    for diagonal in range(DIAGONALS):
        turned = basis
        if diagonal:
            turned = jnp.concatenate([basis[diagonal:], basis[:diagonal]], axis=0)
        products.append(scaled * turned)
    for place, piece in enumerate(split3(jnp.concatenate(products, axis=0))):
        table_ref[place * wide : (place + 1) * wide, :] = piece
    for place, piece in enumerate(split3(scaled)):
        table_ref[rights + place * 16 : rights + place * 16 + 16, :] = piece

    for step in range(steps):
        for which in range(3):
            arrival(which, step).wait()
            if step + AHEAD < steps:
                arrival(which, step + AHEAD).start()
        stars = slice(step * STEP, (step + 1) * STEP)
        quality = quality_ref[stars, :]
        twelfths = jnp.where(
            quality == 0, 12.0, jnp.where(quality == 1, 6.0, jnp.where(quality == 2, 4.0, 3.0))
        )
        weight = jnp.where(valid_ref[stars, :] != 0, twelfths, 0.0)
        grams = dot_nt(table_ref[0:rights, :], weight.astype(BF16))
        gram = grams[0:PAIRS] + (grams[wide : wide + PAIRS] + grams[2 * wide : 2 * wide + PAIRS])
        right = narrow_dots(table_ref, rights, weight * flux_ref[stars, :], 3)
        for chunk in range(CHUNKS):
            lanes = slice(chunk * OWN, (chunk + 1) * OWN)
            out_ref[step * CHUNKS + chunk, 0:PAIRS, :] = gram[:, lanes]
            out_ref[step * CHUNKS + chunk, PAIRS:GRAM_ROWS, :] = right[:, lanes]


def cross_kernel(
    flux_ref, valid_ref, basis_ref, decay_ref, feed_ref, out_ref, decayed_ref, table_ref
):
    cross = BASIS_VECTORS * NOISE_TERMS
    feeds = 2 * cross

    @pl.when(pl.program_id(0) == 0)
    def _():
        log_decay = jnp.log(decay_ref[...])
        count = log_decay.shape[1]
        rows = lax.broadcasted_iota(jnp.int32, (count, count), 0)
        columns = lax.broadcasted_iota(jnp.int32, (count, count), 1)
        suffix = masked_sums(log_decay, rows > columns)
        feed = jnp.exp(suffix) * feed_ref[...]
        whole = jnp.exp(suffix[:, 0:1] + log_decay[:, 0:1])
        decayed_ref[...] = jnp.broadcast_to(whole, (NOISE_TERMS, OWN))
        for k in range(BASIS_VECTORS):
            product = basis_ref[k : k + 1, :] * feed
            for place, piece in enumerate(split3(product)[:2]):
                first = place * cross + k * 16
                table_ref[first : first + 16, :] = piece
        for place, piece in enumerate(split3(feed)):
            table_ref[feeds + place * 16 : feeds + place * 16 + 16, :] = piece

    usable = valid_ref[...] != 0
    flux = flux_ref[...]
    sums = dot_nt(table_ref[0:feeds, :], jnp.where(usable, 1.0, 0.0).astype(BF16))
    crossed = sums[0:cross] + sums[cross : 2 * cross]
    plain = narrow_dots(table_ref, feeds, jnp.where(usable, flux, 0.0), 2)
    for chunk in range(CROSS_CHUNKS):
        lanes = slice(chunk * OWN, (chunk + 1) * OWN)
        out_ref[chunk, 0:16, :] = plain[:, lanes]
        out_ref[chunk, 16:CROSS_ROWS, :] = crossed[:, lanes]


def count_kernel(code_ref, low_ref, near_ref, far_ref):
    entries = 8 * NEIGH
    half, lows_all = near_ref.shape[0], near_ref.shape[2]
    row_code = lax.broadcasted_iota(jnp.int32, (2 * half * 8, entries), 0)
    low_code = lax.broadcasted_iota(jnp.int32, (lows_all, entries), 0)

    def one_half(group):
        code = code_ref[pl.ds(group, 1), :]
        low = low_ref[pl.ds(group, 1), :]
        highs = jnp.where(row_code == code, 1.0, 0.0).astype(BF16)
        lows = jnp.where(low_code == low, 1.0, 0.0).astype(BF16)
        return dot_nt(highs, lows).reshape(2 * half, 8, lows_all)

    def one(step, ignored):
        both = jnp.concatenate([one_half(2 * step), one_half(2 * step + 1)], axis=1).astype(BF16)
        span = pl.ds(pl.multiple_of(step * 16, 16), 16)
        near_ref[:, span, :] = both[:half]
        far_ref[:, span, :] = both[half:]
        return ignored

    lax.fori_loop(0, OWN // 16, one, 0)


def noise_kernel(
    decay_ref, load_ref, feed_ref, basis_ref, high_ref, low_ref, entry_ref, stack_ref
):
    log_decay = jnp.log(decay_ref[...])
    load = load_ref[...]
    feed = feed_ref[...]
    count = log_decay.shape[1]
    rows = lax.broadcasted_iota(jnp.int32, (count, count), 0)
    columns = lax.broadcasted_iota(jnp.int32, (count, count), 1)
    together = (rows // CUT) == (columns // CUT)
    before = masked_sums(log_decay, together & (rows < columns))
    tail = masked_sums(log_decay, together & (rows > columns))
    through = before + log_decay
    cuts = count // CUT
    totals = [through[:, (cut + 1) * CUT - 1 : (cut + 1) * CUT] for cut in range(cuts)]
    lower = lax.broadcasted_iota(jnp.int32, (CUT, CUT), 0) < lax.broadcasted_iota(
        jnp.int32, (CUT, CUT), 1
    )
    high_ref[...] = jnp.zeros_like(high_ref)
    low_ref[...] = jnp.zeros_like(low_ref)

    def keep(u, t, block):
        high = block.astype(BF16)
        span = (slice(u * CUT, (u + 1) * CUT), slice(t * CUT, (t + 1) * CUT))
        high_ref[span] = high
        low_ref[span] = (block - high.astype(F32)).astype(BF16)

    passed = jnp.zeros((NOISE_TERMS, 1), F32)
    entries = []
    for t in range(cuts):
        lanes = slice(t * CUT, (t + 1) * CUT)
        middle = through[:, t * CUT + CUT // 2 - 1 : t * CUT + CUT // 2]
        near_left = feed[:, lanes] * jnp.exp(middle - through[:, lanes])
        near_right = load[:, lanes] * jnp.exp(before[:, lanes] - middle)
        near = dot_tn(left_stack(near_left), right_stack(near_right))
        keep(t, t, jnp.where(lower, near, 0.0))
        far_right = right_stack(load[:, lanes] * jnp.exp(before[:, lanes]))
        between = jnp.zeros((NOISE_TERMS, 1), F32)
        for u in range(t - 1, -1, -1):
            span = slice(u * CUT, (u + 1) * CUT)
            far_left = left_stack(feed[:, span] * jnp.exp(tail[:, span] + between))
            keep(u, t, dot_tn(far_left, far_right))
            between = between + totals[u]
        entries.append(load[:, lanes] * jnp.exp(before[:, lanes] + passed))
        passed = passed + totals[t]
    entry_ref[...] = right_stack(jnp.concatenate(entries, axis=1))
    stack_ref[...] = right_stack(basis_ref[...])


def row_of_pair(i, j):
    apart = (j - i) % BASIS_VECTORS
    if apart < 8 or (apart == 8 and i < 8):
        return apart * BASIS_VECTORS + i
    return ((i - j) % BASIS_VECTORS) * BASIS_VECTORS + j


def eliminate(columns, vector):
    order = BASIS_VECTORS
    columns = list(columns)
    rows = lax.broadcasted_iota(jnp.int32, columns[0].shape, 0)
    scaled, pivots = [], []
    for k in range(order):
        inverse = 1.0 / columns[k][k : k + 1, :]
        factor = jnp.where(rows > k, columns[k] * inverse, 0.0)
        for j in range(k + 1, order):
            columns[j] = columns[j] - factor * columns[j][k : k + 1, :]
        scaled.append(factor)
        pivots.append(inverse)
        if vector is not None:
            vector = vector - factor * vector[k : k + 1, :]
    return scaled, pivots, vector, columns


def back_substitute(vector, uppers, pivots):
    rows = lax.broadcasted_iota(jnp.int32, vector.shape, 0)
    solved = jnp.zeros_like(vector)
    for k in range(BASIS_VECTORS - 1, -1, -1):
        value = vector[k : k + 1, :] * pivots[k]
        vector = vector - uppers[k] * value
        solved = jnp.where(rows == k, value, solved)
    return solved


def solve_kernel(parts_ref, prec_ref, fitted_ref, kept_ref, sums_ref, matrix_ref):
    total = parts_ref[0]
    for part in range(1, parts_ref.shape[0]):
        total = total + parts_ref[part]
    sums_ref[...] = total
    right = total[PAIRS : PAIRS + 16]
    kept_ref[33] = right
    order = BASIS_VECTORS
    for j in range(order):
        for i in range(order):
            row = row_of_pair(i, j)
            matrix_ref[j * order + i : j * order + i + 1, :] = sums_ref[row : row + 1, :]
    rows = lax.broadcasted_iota(jnp.int32, right.shape, 0)
    plain = [matrix_ref[j * order : (j + 1) * order, :] for j in range(order)]
    prec = prec_ref[...]
    ridged = [jnp.where(rows == j, plain[j] + 0.1, plain[j]) for j in range(order)]
    ignored, pivots, reduced, uppers = eliminate(ridged, right)
    fitted = back_substitute(reduced, uppers, pivots)
    for peer in range(fitted_ref.shape[0]):
        fitted_ref[peer] = fitted
    weighted = [jnp.where(rows == j, plain[j] + prec, plain[j]) for j in range(order)]
    factors, pivots, ignored, uppers = eliminate(weighted, None)
    for k in range(order):
        kept_ref[k] = factors[k]
        kept_ref[16 + k] = uppers[k]
        kept_ref[32, k : k + 1, :] = pivots[k]


def listed_sums(table_ref, counts_ref):
    sums = jnp.zeros((48, OWN), F32)
    for place in range(0, table_ref.shape[0], 2):
        wide = jnp.concatenate([table_ref[place], table_ref[place + 1]], axis=1)
        sums = sums + dot_nt(jnp.concatenate(split3(wide), axis=0), counts_ref[place // 2])
    return sums


def near_kernel(near_ref, counts_ref, out_ref):
    out_ref[...] = listed_sums(near_ref, counts_ref)


def map_kernel(begun_ref, far_ref, counts_ref, prec_ref, kept_ref, out_ref):
    prior = begun_ref[...] + listed_sums(far_ref, counts_ref)
    prior_mean = (prior[0:16] + (prior[16:32] + prior[32:48])) * (1.0 / NEIGH)
    vector = kept_ref[33] + prec_ref[...] * prior_mean
    for k in range(BASIS_VECTORS):
        vector = vector - kept_ref[k] * vector[k : k + 1, :]
    uppers = [kept_ref[16 + k] for k in range(BASIS_VECTORS)]
    pivots = [kept_ref[32, k : k + 1, :] for k in range(BASIS_VECTORS)]
    coeffs = back_substitute(vector, uppers, pivots)
    for peer in range(out_ref.shape[0]):
        out_ref[peer] = coeffs


def carry_kernel(rows_ref, crossed_ref, decayed_ref, out_ref):
    owners = rows_ref.shape[0]
    for owner in range(owners):
        coeffs = rows_ref[owner]
        carry = crossed_ref[owner, 0:16, :]
        for k in range(BASIS_VECTORS):
            first = 16 + 16 * k
            carry = carry - coeffs[k : k + 1, :] * crossed_ref[owner, first : first + 16, :]
        out_ref[owner] = carry
    out_ref[owners] = decayed_ref[...]


def level_kernel(own_ref, first_ref, second_ref, third_ref, inner_ref, out_ref):
    place = lax.axis_index("z")
    refs = (own_ref, first_ref, second_ref, third_ref)
    around = len(refs)
    owners = own_ref.shape[0] - 1

    def of_block(block, row):
        value = refs[0][row]
        for back in range(1, around):
            value = jnp.where(lax.rem(place + around - back, around) == block, refs[back][row], value)
        return value

    decays = [of_block(block, owners) for block in range(around)]
    for owner in range(owners):
        state = jnp.zeros((NOISE_TERMS, OWN), F32)
        found = state
        for block in range(around):
            found = jnp.where(place == block, state, found)
            state = state * decays[block] + of_block(block, owner)
        inner_ref[owner] = found
        out_ref[owner] = state
    product = jnp.ones((NOISE_TERMS, OWN), F32)
    before = product
    for block in range(around):
        before = jnp.where(place == block, product, before)
        product = product * decays[block]
    inner_ref[owners] = before
    out_ref[owners] = product


def state_kernel(first_ref, second_ref, third_ref, inner_ref, out_ref):
    owners = out_ref.shape[0]
    for owner in range(owners):
        state = second_ref[owner] + second_ref[owners] * third_ref[owner]
        state = first_ref[owner] + first_ref[owners] * state
        out_ref[owner] = inner_ref[owner] + inner_ref[owners] * state


def local_kernel(flux_ref, valid_ref, rows_ref, stack_ref, high_ref, low_ref, coeffs_ref, out_ref):
    coeffs = jnp.concatenate([rows_ref[chunk] for chunk in range(WHITEN_CHUNKS)], axis=1)
    coeffs_ref[...] = coeffs
    trend = dot_tn(left_stack(coeffs), stack_ref[...])
    first = pl.multiple_of(pl.program_id(0) * WHITEN_STEP, WHITEN_STEP)
    span = pl.ds(first, WHITEN_STEP)
    residual = jnp.where(valid_ref[span, :] != 0, flux_ref[span, :] - trend, 0.0)
    high = residual.astype(BF16)
    low = (residual - high.astype(F32)).astype(BF16)
    count = residual.shape[1]
    for first in range(0, count, 256):
        lanes = slice(first, first + 256)
        upto = slice(0, first + 256)
        local = dot_nn(low[:, upto], high_ref[upto, lanes]) + dot_nn(high[:, upto], low_ref[upto, lanes])
        local = local + dot_nn(high[:, upto], high_ref[upto, lanes])
        out_ref[:, lanes] = residual[:, lanes] - local


def finish_kernel(local_ref, states_ref, entry_ref, scale_ref, out_ref):
    states = jnp.concatenate([states_ref[chunk] for chunk in range(FINISH_CHUNKS)], axis=1)
    incoming = dot_tn(left_stack(states), entry_ref[...])
    first = pl.multiple_of(pl.program_id(0) * FINISH_STEP, FINISH_STEP)
    out_ref[...] = (local_ref[pl.ds(first, FINISH_STEP), :] - incoming) * scale_ref[...]


def vmem():
    return pl.BlockSpec(memory_space=pltpu.VMEM)


def params(mib):
    return pltpu.CompilerParams(vmem_limit_bytes=mib * MIB)


def cost(flops, bytes_accessed):
    return pl.CostEstimate(flops=flops, bytes_accessed=bytes_accessed, transcendentals=0)


def per_device(
    flux, valid, quality, basis, neighbours, prior_prec, decay, load_u, feed_w, inv_diag
):
    stars, cadences = flux.shape
    blocks = stars // OWN
    cadence_axes = ("x", "z")
    place = lax.axis_index(cadence_axes)
    prec = jnp.broadcast_to(prior_prec[:, None], (BASIS_VECTORS, OWN))

    in_hbm = pl.BlockSpec(memory_space=pl.ANY)
    parts = pl.pallas_call(
        gram_kernel,
        in_specs=[in_hbm] * 3 + [vmem()],
        out_specs=vmem(),
        out_shape=jax.ShapeDtypeStruct((blocks, GRAM_ROWS, OWN), F32),
        scratch_shapes=[
            pltpu.VMEM((stars, cadences), F32),
            pltpu.VMEM((stars, cadences), jnp.int32),
            pltpu.VMEM((stars, cadences), jnp.int32),
            pltpu.VMEM((480, cadences), BF16),
            pltpu.SemaphoreType.DMA((3, stars // STEP)),
        ],
        compiler_params=params(58),
        cost_estimate=cost(2 * stars * cadences * 600, 14 * MIB),
        name="gram",
    )(flux, valid, quality, basis)

    parts, later_basis, later_decay, neighbours = lax.optimization_barrier(
        (parts, basis, decay, neighbours)
    )
    listed = lax.dynamic_slice_in_dim(neighbours, place * OWN, OWN, 0).reshape(blocks, -1)
    owner = listed >> 7
    spot = (owner & 15) + 16 * (owner >> 5) + 64 * (((owner >> 4) & 1) ^ lax.axis_index("c"))
    low_bits = (listed & 127) + 128 * (spot & 1)
    code = (spot >> 1) * 8 + lax.broadcasted_iota(jnp.int32, listed.shape, 1) // NEIGH

    cross_spec = pl.BlockSpec((CROSS_STEP, cadences), lambda i: (i, 0))
    table_spec = pl.BlockSpec((16, cadences), lambda i: (0, 0))
    crossed, decayed = pl.pallas_call(
        cross_kernel,
        grid=(stars // CROSS_STEP,),
        in_specs=[cross_spec, cross_spec, table_spec, table_spec, table_spec],
        out_specs=[
            pl.BlockSpec((CROSS_CHUNKS, CROSS_ROWS, OWN), lambda i: (i, 0, 0)),
            pl.BlockSpec((NOISE_TERMS, OWN), lambda i: (0, 0)),
        ],
        out_shape=[
            jax.ShapeDtypeStruct((blocks, CROSS_ROWS, OWN), F32),
            jax.ShapeDtypeStruct((NOISE_TERMS, OWN), F32),
        ],
        scratch_shapes=[pltpu.VMEM((560, cadences), BF16)],
        compiler_params=params(58),
        cost_estimate=cost(2 * stars * cadences * 800, 16 * MIB),
        name="cross",
    )(flux, valid, later_basis, later_decay, feed_w)
    parts = lax.all_to_all(parts, cadence_axes, 0, 0, tiled=True)
    near_counts, far_counts = pl.pallas_call(
        count_kernel,
        in_specs=[vmem(), vmem()],
        out_specs=[vmem()] * 2,
        out_shape=[jax.ShapeDtypeStruct((32, OWN, 256), BF16)] * 2,
        compiler_params=params(16),
        cost_estimate=cost(4 << 30, 4 * MIB),
        name="count",
    )(code, low_bits)
    parts, crossed, decayed, near_counts, far_counts = lax.optimization_barrier(
        (parts, crossed, decayed, near_counts, far_counts)
    )

    nearby = ("y", "x", "z")
    copies = jax.ShapeDtypeStruct((lax.axis_size(nearby), 16, OWN), F32)
    fitted, kept = pl.pallas_call(
        solve_kernel,
        in_specs=[vmem()] * 2,
        out_specs=[vmem()] * 2,
        out_shape=[copies, jax.ShapeDtypeStruct((34, 16, OWN), F32)],
        scratch_shapes=[pltpu.VMEM((GRAM_ROWS, OWN), F32), pltpu.VMEM((256, OWN), F32)],
        compiler_params=params(16),
        cost_estimate=cost(1 << 20, 2 * MIB),
        name="solve",
    )(parts, prec)

    near = lax.all_to_all(fitted, nearby, 0, 0, tiled=True)
    near, last_decay, last_basis = lax.optimization_barrier((near, decay, basis))
    far = lax.ppermute(near, "c", [(0, 1), (1, 0)])
    begun = pl.pallas_call(
        near_kernel,
        in_specs=[vmem()] * 2,
        out_specs=vmem(),
        out_shape=jax.ShapeDtypeStruct((48, OWN), F32),
        compiler_params=params(16),
        cost_estimate=cost(1 << 28, 3 * MIB),
        name="near",
    )(near, near_counts)

    high, low, entry, stack = pl.pallas_call(
        noise_kernel,
        in_specs=[vmem()] * 4,
        out_specs=[vmem()] * 4,
        out_shape=[
            jax.ShapeDtypeStruct((cadences, cadences), BF16),
            jax.ShapeDtypeStruct((cadences, cadences), BF16),
            jax.ShapeDtypeStruct((96, cadences), BF16),
            jax.ShapeDtypeStruct((96, cadences), BF16),
        ],
        compiler_params=params(16),
        cost_estimate=cost(2 << 30, 2 * MIB),
        name="noise",
    )(last_decay, load_u, feed_w, last_basis)
    far, begun, high, low, entry, stack = lax.optimization_barrier(
        (far, begun, high, low, entry, stack)
    )
    rows = pl.pallas_call(
        map_kernel,
        in_specs=[vmem()] * 5,
        out_specs=vmem(),
        out_shape=jax.ShapeDtypeStruct((blocks, 16, OWN), F32),
        compiler_params=params(16),
        cost_estimate=cost(1 << 28, 6 * MIB),
        name="map",
    )(begun, far, far_counts, prec, kept)
    rows = lax.all_to_all(rows, cadence_axes, 0, 0, tiled=True)

    block_shape = jax.ShapeDtypeStruct((blocks + 1, 16, OWN), F32)
    carries = pl.pallas_call(
        carry_kernel,
        in_specs=[vmem()] * 3,
        out_specs=vmem(),
        out_shape=block_shape,
        compiler_params=params(16),
        cost_estimate=cost(1 << 24, 3 * MIB),
        name="local_carry",
    )(rows, crossed, decayed)
    along_z, along_x = lax.axis_size("z"), lax.axis_size("x")
    rings = [
        lax.ppermute(carries, "z", [(i, (i + back) % along_z) for i in range(along_z)])
        for back in range(1, along_z)
    ]
    inner, lines = pl.pallas_call(
        level_kernel,
        in_specs=[vmem()] * 4,
        out_specs=[vmem()] * 2,
        out_shape=[block_shape] * 2,
        compiler_params=params(16),
        cost_estimate=cost(1 << 20, MIB),
        name="level",
    )(carries, *rings)
    part_spec = pl.BlockSpec((WHITEN_CHUNKS, 16, OWN), lambda i: (i, 0, 0))
    tall_spec = pl.BlockSpec((WHITEN_STEP, cadences), lambda i: (i, 0))
    coeffs, local = pl.pallas_call(
        local_kernel,
        grid=(stars // WHITEN_STEP,),
        in_specs=[vmem(), vmem(), part_spec] + [vmem()] * 3,
        out_specs=[pl.BlockSpec((16, WHITEN_STEP), lambda i: (0, i)), tall_spec],
        out_shape=[
            jax.ShapeDtypeStruct((16, stars), F32),
            jax.ShapeDtypeStruct((stars, cadences), F32),
        ],
        compiler_params=params(24),
        cost_estimate=cost(2 * stars * cadences * 1500, 14 * MIB),
        name="local",
    )(flux, valid, rows, stack, high, low)
    earlier = [
        lax.ppermute(lines, "x", [(i, i + back) for i in range(along_x - back)])
        for back in range(1, along_x)
    ]
    states = pl.pallas_call(
        state_kernel,
        in_specs=[vmem()] * 4,
        out_specs=vmem(),
        out_shape=jax.ShapeDtypeStruct((blocks, 16, OWN), F32),
        compiler_params=params(16),
        cost_estimate=cost(1 << 20, MIB),
        name="state",
    )(*earlier, inner)

    whitened = pl.pallas_call(
        finish_kernel,
        grid=(stars // FINISH_STEP,),
        in_specs=[
            vmem(),
            pl.BlockSpec((FINISH_CHUNKS, 16, OWN), lambda i: (i, 0, 0)),
            vmem(),
            vmem(),
        ],
        out_specs=pl.BlockSpec((FINISH_STEP, cadences), lambda i: (i, 0)),
        out_shape=jax.ShapeDtypeStruct((stars, cadences), F32),
        compiler_params=params(16),
        cost_estimate=cost(2 * stars * cadences * 100, 9 * MIB),
        name="finish",
    )(local, states, entry, inv_diag[None, :])
    return coeffs.T, whitened


def solution(mesh):
    devices = mesh.devices
    split = Mesh(devices.reshape(devices.shape[0] // 2, 2, 4, devices.shape[1] // 4), ("y", "c", "x", "z"))
    tm = ("x", "z")
    star = ("y", "c")
    in_specs = (
        P(star, tm),
        P(star, tm),
        P(star, tm),
        P(None, tm),
        P(star, None),
        P(),
        P(None, tm),
        P(None, tm),
        P(None, tm),
        P(tm),
    )
    out_specs = (P(star, None), P(star, tm))
    return jax.shard_map(
        per_device, mesh=split, in_specs=in_specs, out_specs=out_specs, check_vma=False
    )
```
